512 devices in a mesh: seq: 32 (over x, y_lo, core), ch: 16 (over y_hi, z).
Axes of the slice: x: 4, y: 8 (y_hi: 2, y_lo: 4; y = y_hi * 4 + y_lo), z: 8, core: 2. Of those that a mesh axis runs over, the one named last changes fastest.
Arguments:
- inputs: bfloat16 [4096, 4096], P('seq', 'ch'), may hold values from -6 to 6
- out_grad: bfloat16 [4096, 4096], P('seq', 'ch'), may hold values from -6 to 6
- embed_weight: float32 [32, 64], replicated, may hold values from -3 to 3
- filter_weight: float32 [64, 4096], P(None, 'ch'), may hold values from -0.01171875 to 0.01171875
- decay_rate: float32 [4096], P('ch'), may hold values from 0.1 to 128
- skip_gain: float32 [4096], P('ch'), may hold values from 0.5 to 1.5
Outputs:
- signal_grad: bfloat16 [4096, 4096], P('seq', 'ch')
- filter_grad: float32 [64, 4096], P(None, 'ch')
- embed_grad: float32 [32, 64], replicated
The draws below stay inside these ranges and needn't reach their ends.
All inputs are finite; a program needn't handle non-finite values.
Results may differ from the reference program's by a relative error of at most 0.002.
Values may be sent and summed in bfloat16 or wider, within the bound.
A program may use at most 64 MiB of HBM per device.

```python
import math
import jax
import jax.numpy as jnp
from jax import lax

CHANNELS = 4096
EMBED = 32
FHID = 64
TOK_DEV = 128
TOKENS = 4096
N_SEQ = 32


def level_of(key, dims, split, low, high):
    def one(position, blocks):
        draws = jax.random.uniform(jax.random.fold_in(jax.random.fold_in(key, 6), position), (blocks,), jnp.float32, low / len(split), high / len(split))
        return jnp.repeat(jnp.exp(draws), dims[position] // blocks).reshape((-1,) + (1,) * (len(dims) - position - 1))

    gain = one(*split[0])
    for cut in split[1:]:
        gain = gain * one(*cut)
    return gain


def scatter_about(key, dims, deviation, reach, pieces=(), kind=jnp.bfloat16):
    gain = level_of(key, dims, pieces, -0.22, 0.18) if pieces else 1.0
    result = jax.random.normal(key, dims, jnp.float32) * deviation * gain
    return jnp.minimum(jnp.maximum(result, -reach), reach).astype(kind)


def setup_inputs(seed: int = 0) -> dict:
    splits = jax.random.split(jax.random.key(seed), 7)
    inputs = scatter_about(splits[0], (TOKENS, CHANNELS), 1.0, 6.0, ((0, 32), (1, 16)))
    out_grad = scatter_about(splits[1], (TOKENS, CHANNELS), 1.0, 6.0, ((0, 32), (1, 16)))
    embed_weight = scatter_about(splits[2], (EMBED, FHID), 0.5, 3.0, (), jnp.float32)
    filter_weight = scatter_about(splits[3], (FHID, CHANNELS), (FHID * TOK_DEV * N_SEQ) ** -0.5, 0.01171875, ((1, 16),), jnp.float32)
    decay_rate = jnp.clip(jnp.exp(math.log(128.0) - 7.1546153 * jax.random.uniform(splits[4], (CHANNELS,), jnp.float32) ** level_of(splits[4], (CHANNELS,), ((0, 16),), -0.2, 0.2)), 0.1, 128.0)
    skip_gain = jnp.clip(0.5 + 1.0 * jax.random.uniform(splits[5], (CHANNELS,), jnp.float32) ** level_of(splits[5], (CHANNELS,), ((0, 16),), -0.2, 0.2), 0.5, 1.5)
    return dict(inputs=inputs, out_grad=out_grad, embed_weight=embed_weight, filter_weight=filter_weight, decay_rate=decay_rate, skip_gain=skip_gain)


HIGHEST = lax.Precision.HIGHEST

def correlate(grad_block, input_block, filter_block):
    length = grad_block.shape[0]
    padded_len = 2 * length
    grad_spec = jnp.fft.rfft(grad_block.astype(jnp.float32), n=padded_len, axis=0)
    input_spec = jnp.fft.rfft(input_block.astype(jnp.float32), n=padded_len, axis=0)
    filter_spec = jnp.fft.rfft(filter_block.astype(jnp.float32), n=padded_len, axis=0)
    conv_grad = jnp.fft.irfft(grad_spec * jnp.conj(filter_spec), n=padded_len, axis=0)[:length]
    lag_grad = jnp.fft.irfft(grad_spec * jnp.conj(input_spec), n=padded_len, axis=0)[:length]
    return (conv_grad.astype(jnp.float32), lag_grad.astype(jnp.float32))

def reference(inputs, out_grad, embed_weight, filter_weight, decay_rate, skip_gain):
    length = TOKENS
    positions = jnp.arange(length, dtype=jnp.int32)
    half_count = EMBED // 2
    phase_num = positions[:, None] * (jnp.arange(half_count, dtype=jnp.int32) + 1)[None, :] % length
    angles = phase_num.astype(jnp.float32) * (2 * math.pi / length)
    features = jnp.concatenate([jnp.sin(angles), jnp.cos(angles)], axis=1)
    preact = jnp.dot(features, embed_weight, precision=HIGHEST)
    active = jnp.sin(preact)
    filter_base = jnp.dot(active, filter_weight, precision=HIGHEST)
    decays = jnp.exp(-decay_rate[None, :] * positions[:, None].astype(jnp.float32) / length)
    filter_rows = (filter_base * decays).astype(jnp.bfloat16)

    def split_blocks(array):
        return array.reshape(length, CHANNELS // 256, 256).transpose(1, 0, 2)

    def join_blocks(array):
        return array.transpose(1, 0, 2).reshape(length, CHANNELS)

    def one_block(item):
        return correlate(item[0], item[1], item[2])
    conv_blocks, lag_blocks = lax.map(one_block, (split_blocks(out_grad), split_blocks(inputs), split_blocks(filter_rows)))
    conv_grad = join_blocks(conv_blocks)
    lag_grad = join_blocks(lag_blocks)
    signal_grad = (conv_grad + skip_gain[None, :] * out_grad.astype(jnp.float32)).astype(jnp.bfloat16)
    base_grad = lag_grad * decays
    filter_grad = jnp.dot(active.T, base_grad, precision=HIGHEST) / length
    hidden_grad = jnp.dot(base_grad, filter_weight.T, precision=HIGHEST)
    embed_grad = jnp.dot(features.T, hidden_grad * jnp.cos(preact), precision=HIGHEST) / math.sqrt(length)
    return (signal_grad, filter_grad, embed_grad)
```

```python
import functools
import math

import jax
import jax.numpy as jnp
import ml_dtypes
import numpy as np
from jax import lax
from jax.experimental import pallas as pl
from jax.experimental.pallas import tpu as pltpu
from jax.sharding import PartitionSpec as P

F32 = jnp.float32
BF16 = jnp.bfloat16
BLOCKS = 32
ROWS = 128
OWN = 8
GROUPS = 16
HID = 64
EMB = 32
LENGTH = BLOCKS * ROWS
PADDED = 2 * LENGTH
ROOT_HALF = math.sqrt(0.5)
OUTER = (
    [8 * m for m in range(5)]
    + [4 + 8 * m for m in range(4)]
    + [f + 8 * m for f in (1, 2, 3) for m in range(8)]
)
KEPT = len(OUTER)
PLACE = {k: n for n, k in enumerate(OUTER)}


def dot(a, b, contract=((1,), (0,))):
    return lax.dot_general(a, b, (contract, ((), ())), preferred_element_type=F32)


def halves(x):
    high = x.astype(BF16)
    return high, (x - high.astype(F32)).astype(BF16)


def np_halves(x):
    high = x.astype(ml_dtypes.bfloat16)
    low = (x - high.astype(np.float64)).astype(ml_dtypes.bfloat16)
    return high, low


@functools.cache
def tables():
    t = np.arange(LENGTH, dtype=np.int64)
    e = np.arange(EMB // 2, dtype=np.int64) + 1
    angle = (e[:, None] * t[None, :] % LENGTH).astype(np.float64) * (2 * math.pi / LENGTH)
    high, low = np_halves(np.concatenate([np.sin(angle), np.cos(angle)], axis=0))
    feats = np.concatenate([high, low, high], axis=0)
    n = np.arange(ROWS, dtype=np.int64)
    angle = (n[:, None] * n[None, :] % ROWS).astype(np.float64) * (2 * math.pi / ROWS)
    cos, sin = np.cos(angle), np.sin(angle)
    forward = np.block([[cos, -sin], [sin, cos]])
    back = np.block([[cos, sin], [-sin, cos]]) * (2.0 / PADDED)
    inner = np.stack([*np_halves(forward), *np_halves(back)])
    outer = np.array(OUTER, dtype=np.int64)
    angle = (outer[:, None] * n[None, :]).astype(np.float64) * (2 * math.pi / PADDED)
    turn = np.stack([np.cos(angle), np.sin(angle)]).astype(np.float32)
    turn = np.ascontiguousarray(np.broadcast_to(turn[:, :, None, :], (2, KEPT, OWN, ROWS)))
    return feats, inner, turn


HALF_TURN = (3.140625, 9.67025756835937500e-4, 6.2771141529083251953e-7, 1.2154201256553420e-10)
SIN_SERIES = (1.0, -1 / 6, 1 / 120, -1 / 5040, 1 / 362880, -1 / 39916800)
COS_SERIES = (1.0, -1 / 2, 1 / 24, -1 / 720, 1 / 40320, -1 / 3628800, 1 / 479001600)


def series(coefs, x):
    total = jnp.full_like(x, coefs[-1])
    for coef in coefs[-2::-1]:
        total = total * x + coef
    return total


def sine_cosine(x):
    turns = jnp.round(x * (1 / math.pi))
    rest = x
    for part in HALF_TURN[:3]:
        rest = rest - turns * part
    half = turns * 0.5
    sign = 1.0 - 4.0 * jnp.abs(half - jnp.round(half))
    square = rest * rest
    return sign * rest * series(SIN_SERIES, square), sign * series(COS_SERIES, square)


def c_add(a, b):
    return tuple(p if q is None else q if p is None else p + q for p, q in zip(a, b))


def c_neg(a):
    return tuple(None if p is None else -p for p in a)


def c_sub(a, b):
    return tuple(
        p if q is None else -q if p is None else p - q for p, q in zip(a, b)
    )


def c_turn(a, number, count):
    number = number % count
    if number == 0:
        return a
    if 2 * number == count:
        return c_neg(a)
    re, im = a
    if 4 * number == count:
        return (None if im is None else -im, re)
    if 4 * number == 3 * count:
        return (im, None if re is None else -re)
    cos, sin = math.cos(2 * math.pi * number / count), math.sin(2 * math.pi * number / count)
    if im is None:
        return (re * cos, re * sin)
    if 8 * number == count:
        return ((re - im) * ROOT_HALF, (re + im) * ROOT_HALF)
    if 8 * number == 7 * count:
        return ((re + im) * ROOT_HALF, (im - re) * ROOT_HALF)
    if 8 * number == 3 * count:
        return ((re + im) * -ROOT_HALF, (re - im) * ROOT_HALF)
    if 8 * number == 5 * count:
        return ((im - re) * ROOT_HALF, (re + im) * -ROOT_HALF)
    return (re * cos - im * sin, re * sin + im * cos)


def transform(values, sign):
    count = len(values)
    if count == 1:
        return list(values)
    even, odd = transform(values[::2], sign), transform(values[1::2], sign)
    odd = [c_turn(v, sign * k, count) for k, v in enumerate(odd)]
    return [c_add(a, b) for a, b in zip(even, odd)] + [c_sub(a, b) for a, b in zip(even, odd)]


def outer_forward(x):
    parts = [[None] * 8 for _ in range(5)]
    for b in range(8):
        x0, x1, x2, x3 = x[b], x[8 + b], x[16 + b], x[24 + b]
        plus, minus, other, differ = x0 + x2, x0 - x2, x1 + x3, x1 - x3
        part, whole = differ * ROOT_HALF, other * ROOT_HALF
        parts[0][b] = (plus + other, None)
        parts[4][b] = (plus - other, None)
        parts[2][b] = (minus, -differ)
        parts[1][b] = (x0 + part, -(x2 + whole))
        parts[3][b] = (x0 - part, x2 - whole)
    found = {}
    for f in range(5):
        turned = [c_turn(v, -b * f, 64) for b, v in enumerate(parts[f])]
        for m, v in enumerate(transform(turned, -1)):
            found[f + 8 * m] = v
    return [found[k] for k in OUTER]


def outer_back(z):
    z = {k: z[n] for n, k in enumerate(OUTER)}
    s = ROOT_HALF
    ends, sides = z[0][0] + z[32][0], z[0][0] - z[32][0]
    (r1, i1), (r2, i2), (r3, i3) = z[8], z[16], z[24]
    one, two = s * ((r1 - i1) - (r3 + i3)), s * ((r3 - i3) - (r1 + i1))
    rsum, idiff = r1 + r3, i3 - i1
    v0 = [
        ends + r2 + rsum,
        sides - i2 + one,
        ends - r2 + idiff,
        sides + i2 + two,
        ends + r2 - rsum,
        sides - i2 - one,
        ends - r2 - idiff,
        sides + i2 - two,
    ]
    quarter = [z[4 + 8 * m] for m in range(4)]
    even = transform(quarter, 1)
    odd = transform([c_turn(v, m, 8) for m, v in enumerate(quarter)], 1)
    v4 = []
    for b in range(8):
        re, im = (odd if b % 2 else even)[b // 2]
        angle = 2 * math.pi * b / 16
        v4.append(re if b == 0 else re * math.cos(angle) - im * math.sin(angle))
    v1, v2, v3 = (
        [c_turn(v, b * f, 64) for b, v in enumerate(transform([z[f + 8 * m] for m in range(8)], 1))]
        for f in (1, 2, 3)
    )
    y = [None] * BLOCKS
    for b in range(8):
        (r1, i1), (r2, i2), (r3, i3) = v1[b], v2[b], v3[b]
        ends, sides = v0[b] + v4[b], v0[b] - v4[b]
        y[b] = ends + r2 + (r1 + r3)
        y[8 + b] = sides - i2 + s * ((r1 - i1) - (r3 + i3))
        y[16 + b] = ends - r2 + (i3 - i1)
        y[24 + b] = sides + i2 + s * ((r3 - i3) - (r1 + i1))
    return y


def spread(load, turn, spec):
    for n, (re, im) in enumerate(outer_forward([load(b) for b in range(BLOCKS)])):
        cos, sin = turn[0, n], turn[1, n]
        spec[n, :, :ROWS] = re * cos if im is None else re * cos + im * sin
        spec[n, :, ROWS:] = -(re * sin) if im is None else im * cos - re * sin


def gather(spec, turn):
    z = []
    for n, k in enumerate(OUTER):
        re, im, cos, sin = spec[n, :, :ROWS], spec[n, :, ROWS:], turn[0, n], turn[1, n]
        re, im = re * cos - im * sin, im * cos + re * sin
        z.append((re * 0.5, im * 0.5) if k in (0, 32) else (re, im))
    return outer_back(z)


def inner_pass(x, high, low):
    x_high, x_low = halves(x)
    return dot(x_high, high) + dot(x_low, high) + dot(x_high, low)


def inner_forward(spec, inner):
    x = spec[...].reshape(KEPT * OWN, 2 * ROWS)
    spec[...] = inner_pass(x, inner[0], inner[1]).reshape(KEPT, OWN, 2 * ROWS)


def inner_back(left, right, spec, inner):
    lr, li = left[:, :, :ROWS], left[:, :, ROWS:]
    rr, ri = right[:, :, :ROWS], right[:, :, ROWS:]
    re = (lr * rr + li * ri).reshape(KEPT * OWN, ROWS)
    im = (li * rr - lr * ri).reshape(KEPT * OWN, ROWS)
    x = jnp.concatenate([re, im], axis=1)
    spec[...] = inner_pass(x, inner[2], inner[3]).reshape(KEPT, OWN, 2 * ROWS)


def kernel(
    u_in, g_in, ew_in, fw_in, rate_in, gain_in, feats_in, inner_in, turn_in,
    sig_out, fgrad_out, egrad_out,
    u, g, ew, fw, rate_row, gain_row, feats, inner, turn,
    send_x, recv_x, own_par, pre, active, slopes, base, filt, decays,
    spec_f, spec_u, spec_g, spec_y, bg, q,
    send_s, recv_s, send_f, recv_f, part1, recv1, part2, recv2, part3, recv3,
    in_sem, send_sem, recv_sem,
):
    me, group = lax.axis_index("seq"), lax.axis_index("ch")
    barrier = pltpu.get_barrier_semaphore()

    def greet(axis, own, count):
        @pl.loop(1, count)
        def _(d):
            pl.semaphore_signal(barrier, inc=1, device_id={axis: lax.rem(own + d, count)})

    greet("seq", me, BLOCKS)
    greet("ch", group, GROUPS)

    pairs = (
        (u_in, u), (g_in, g), (ew_in, ew), (fw_in, fw), (rate_in, rate_row), (gain_in, gain_row),
        (feats_in, feats), (inner_in, inner), (turn_in, turn),
    )
    loads = [pltpu.make_async_copy(a, b, in_sem.at[n]) for n, (a, b) in enumerate(pairs)]
    for load in loads:
        load.start()

    def send(n, axis, own, count, source, target):
        @pl.loop(1, count)
        def _(d):
            peer = lax.rem(own + d, count)
            pltpu.make_async_remote_copy(
                src_ref=source(peer),
                dst_ref=target.at[own],
                send_sem=send_sem.at[n],
                recv_sem=recv_sem.at[n],
                device_id={axis: peer},
            ).start()

    def wait(sem, n, ref, count):
        part = ref.at[pl.ds(0, count)]
        pltpu.make_async_copy(part, part, sem.at[n]).wait()

    loads[0].wait()
    loads[1].wait()
    send_x[...] = jnp.concatenate(
        [x[...].astype(F32).T.reshape(BLOCKS, OWN, ROWS) for x in (u, g)], axis=1
    ).astype(BF16)
    pl.semaphore_wait(barrier, BLOCKS + GROUPS - 2)
    send(0, "seq", me, BLOCKS, lambda peer: send_x.at[peer], recv_x)
    recv_x[pl.ds(me, 1)] = send_x[pl.ds(me, 1)]

    for load in loads[2:]:
        load.wait()
    own_par[:, :HID] = fw[...].T
    own_par[:, HID : HID + 8] = jnp.broadcast_to(rate_row[...], (8, BLOCKS * OWN)).T
    own_par[:, HID + 8 : HID + 16] = jnp.broadcast_to(gain_row[...], (8, BLOCKS * OWN)).T
    par = own_par[pl.ds(pl.multiple_of(me * OWN, OWN), OWN), :]
    weight = par[:, :HID]
    rate = jnp.broadcast_to(par[:, HID : HID + 1], (OWN, ROWS))
    gain = jnp.broadcast_to(par[:, HID + 8 : HID + 9], (OWN, ROWS))
    w_high, w_low = halves(weight)

    e_high, e_low = halves(ew[...].T)
    pre[...] = dot(jnp.concatenate([e_high, e_high, e_low], axis=1), feats[...])

    @pl.loop(0, LENGTH // 256)
    def _(n):
        columns = pl.ds(pl.multiple_of(n * 256, 256), 256)
        sine, cosine = sine_cosine(pre[:, columns])
        high, low = halves(sine)
        active[:HID, columns] = high
        active[HID:, columns] = low
        slopes[:, columns] = cosine

    stacked = jnp.concatenate(
        [
            jnp.concatenate([w_high.astype(F32), w_high.astype(F32)], axis=1),
            jnp.concatenate([w_low.astype(F32), jnp.zeros((OWN, HID), F32)], axis=1),
        ],
        axis=0,
    ).astype(BF16)
    base[...] = dot(stacked, active[...])

    lanes = lax.broadcasted_iota(jnp.int32, (OWN, ROWS), 1)
    for b in range(BLOCKS):
        columns = slice(b * ROWS, (b + 1) * ROWS)
        decay = jnp.exp(-rate * (lanes + b * ROWS).astype(F32) / LENGTH)
        decays[b] = decay
        value = (base[:OWN, columns] + base[OWN:, columns]) * decay
        filt[b] = value.astype(BF16).astype(F32)
    spread(lambda b: filt[b], turn, spec_f)
    inner_forward(spec_f, inner)

    wait(recv_sem, 0, recv_x, BLOCKS - 1)
    spread(lambda b: recv_x[b].astype(F32)[:OWN], turn, spec_u)
    spread(lambda b: recv_x[b].astype(F32)[OWN:], turn, spec_g)
    inner_forward(spec_u, inner)
    inner_forward(spec_g, inner)

    inner_back(spec_g, spec_u, spec_y, inner)
    for b, lag in enumerate(gather(spec_y, turn)):
        bg[:, b * ROWS : (b + 1) * ROWS] = lag * decays[b]
    b_high, b_low = halves(bg[...])
    left = jnp.concatenate([w_high, w_low, w_high], axis=0)
    right = jnp.concatenate([b_high, b_high, b_low], axis=0)
    q_high, q_low = halves(dot(left, right, ((0,), (0,))) * slopes[...])
    q[:HID] = q_high
    q[HID:] = q_low
    parts = dot(feats[: 2 * EMB], q[...], ((1,), (1,)))
    embed = parts[:EMB, :HID] + parts[:EMB, HID:] + parts[EMB:, :HID]
    part1[...] = jnp.concatenate([embed[:GROUPS], embed[GROUPS:]], axis=1).reshape(GROUPS, 1, ROWS)
    send(1, "ch", group, GROUPS, lambda peer: part1.at[peer], recv1)
    recv1[pl.ds(group, 1)] = part1[pl.ds(group, 1)]

    inner_back(spec_g, spec_f, spec_y, inner)
    for b, conv in enumerate(gather(spec_y, turn)):
        send_s[b] = (conv + gain * recv_x[b].astype(F32)[OWN:]).astype(BF16)
    send(2, "seq", me, BLOCKS, lambda peer: send_s.at[peer], recv_s)
    recv_s[pl.ds(me, 1)] = send_s[pl.ds(me, 1)]

    wait(recv_sem, 1, recv1, GROUPS - 1)
    part2[...] = jnp.sum(recv1[...], axis=0, keepdims=True)
    send(3, "seq", me, BLOCKS, lambda peer: part2.at[0], recv2)
    recv2[pl.ds(me, 1)] = part2[...]

    parts = dot(jnp.concatenate([b_high, b_low], axis=0), active[...], ((1,), (1,)))
    fgrad = (parts[:OWN, :HID] + parts[:OWN, HID:] + parts[OWN:, :HID]) * (1.0 / LENGTH)
    send_f[0] = jnp.concatenate([fgrad[: OWN // 2], fgrad[OWN // 2 :]], axis=1)
    send(4, "seq", me, BLOCKS, lambda peer: send_f.at[0], recv_f)
    recv_f[pl.ds(me, 1)] = send_f[...]

    wait(recv_sem, 3, recv2, BLOCKS - 1)
    part3[...] = jnp.sum(recv2[...], axis=0, keepdims=True) * (1.0 / math.sqrt(LENGTH))
    send(5, "ch", group, GROUPS, lambda peer: part3.at[0], recv3)
    recv3[pl.ds(group, 1)] = part3[...]

    wait(recv_sem, 2, recv_s, BLOCKS - 1)
    sig_out[...] = recv_s[...].astype(F32).reshape(BLOCKS * OWN, ROWS).T.astype(BF16)

    wait(recv_sem, 4, recv_f, BLOCKS - 1)
    pieces = recv_f[...]
    fgrad_out[...] = (
        jnp.concatenate([pieces[:, :, :HID], pieces[:, :, HID:]], axis=1).reshape(BLOCKS * OWN, HID).T
    )

    wait(recv_sem, 5, recv3, GROUPS - 1)
    embed = recv3[...].reshape(GROUPS, ROWS)
    egrad_out[:GROUPS] = embed[:, :HID]
    egrad_out[GROUPS:] = embed[:, HID:]

    wait(send_sem, 0, send_x, BLOCKS - 1)
    wait(send_sem, 1, part1, GROUPS - 1)
    wait(send_sem, 2, send_s, BLOCKS - 1)
    wait(send_sem, 3, recv2, BLOCKS - 1)
    wait(send_sem, 4, recv_f, BLOCKS - 1)
    wait(send_sem, 5, recv3, GROUPS - 1)


def local(inputs, out_grad, embed_weight, filter_weight, decay_rate, skip_gain):
    channels = inputs.shape[1]
    feats, inner, turn = tables()
    operands = (
        inputs,
        out_grad,
        embed_weight,
        filter_weight,
        decay_rate.reshape(1, channels),
        skip_gain.reshape(1, channels),
        jnp.asarray(feats),
        jnp.asarray(inner),
        jnp.asarray(turn),
    )
    vmem = pltpu.VMEM
    return pl.pallas_call(
        kernel,
        out_shape=(
            jax.ShapeDtypeStruct((ROWS, channels), BF16),
            jax.ShapeDtypeStruct((HID, channels), F32),
            jax.ShapeDtypeStruct((EMB, HID), F32),
        ),
        in_specs=[pl.BlockSpec(memory_space=pl.ANY)] * len(operands),
        out_specs=[pl.BlockSpec(memory_space=pltpu.VMEM)] * 3,
        scratch_shapes=[vmem(x.shape, x.dtype) for x in operands]
        + [
            vmem((BLOCKS, 2 * OWN, ROWS), BF16),
            vmem((BLOCKS, 2 * OWN, ROWS), BF16),
            vmem((channels, ROWS), F32),
            vmem((HID, LENGTH), F32),
            vmem((2 * HID, LENGTH), BF16),
            vmem((HID, LENGTH), F32),
            vmem((2 * OWN, LENGTH), F32),
            vmem((BLOCKS, OWN, ROWS), F32),
            vmem((BLOCKS, OWN, ROWS), F32),
            vmem((KEPT, OWN, 2 * ROWS), F32),
            vmem((KEPT, OWN, 2 * ROWS), F32),
            vmem((KEPT, OWN, 2 * ROWS), F32),
            vmem((KEPT, OWN, 2 * ROWS), F32),
            vmem((OWN, LENGTH), F32),
            vmem((2 * HID, LENGTH), BF16),
            vmem((BLOCKS, OWN, ROWS), BF16),
            vmem((BLOCKS, OWN, ROWS), BF16),
            vmem((1, OWN // 2, ROWS), F32),
            vmem((BLOCKS, OWN // 2, ROWS), F32),
            vmem((GROUPS, 1, ROWS), F32),
            vmem((GROUPS, 1, ROWS), F32),
            vmem((1, 1, ROWS), F32),
            vmem((BLOCKS, 1, ROWS), F32),
            vmem((1, 1, ROWS), F32),
            vmem((GROUPS, 1, ROWS), F32),
            pltpu.SemaphoreType.DMA((len(operands),)),
            pltpu.SemaphoreType.DMA((6,)),
            pltpu.SemaphoreType.DMA((6,)),
        ],
        compiler_params=pltpu.CompilerParams(
            collective_id=0, has_side_effects=True, vmem_limit_bytes=40 * 1024 * 1024
        ),
        name="hyena_backward",
    )(*operands)


def solution(mesh):
    return jax.shard_map(
        local,
        mesh=mesh,
        in_specs=(P("seq", "ch"), P("seq", "ch"), P(), P(None, "ch"), P("ch"), P("ch")),
        out_specs=(P("seq", "ch"), P(None, "ch"), P()),
        check_vma=False,
    )
```

```python
import functools
import math

import jax
import jax.numpy as jnp
import ml_dtypes
import numpy as np
from jax import lax
from jax.experimental import pallas as pl
from jax.experimental.pallas import tpu as pltpu
from jax.sharding import PartitionSpec as P

F32 = jnp.float32
BF16 = jnp.bfloat16
BLOCKS = 32
ROWS = 128
OWN = 8
RUN = 4
CORES = 2
PLACES = 8
RING = 8
HID = 64
EMB = 32
LENGTH = BLOCKS * ROWS
PADDED = 2 * LENGTH
ROOT_HALF = math.sqrt(0.5)
OUTER = (
    [8 * m for m in range(5)]
    + [4 + 8 * m for m in range(4)]
    + [f + 8 * m for f in (1, 2, 3) for m in range(8)]
)
KEPT = len(OUTER)
PLACE = {k: n for n, k in enumerate(OUTER)}


def dot(a, b, contract=((1,), (0,))):
    return lax.dot_general(a, b, (contract, ((), ())), preferred_element_type=F32)


def halves(x):
    high = x.astype(BF16)
    return high, (x - high.astype(F32)).astype(BF16)


def np_halves(x):
    high = x.astype(ml_dtypes.bfloat16)
    low = (x - high.astype(np.float64)).astype(ml_dtypes.bfloat16)
    return high, low


@functools.cache
def tables():
    t = np.arange(LENGTH, dtype=np.int64)
    e = np.arange(EMB // 2, dtype=np.int64) + 1
    angle = (e[:, None] * t[None, :] % LENGTH).astype(np.float64) * (2 * math.pi / LENGTH)
    high, low = np_halves(np.concatenate([np.sin(angle), np.cos(angle)], axis=0))
    feats = np.concatenate([high, low, high], axis=0)
    n = np.arange(ROWS, dtype=np.int64)
    angle = (n[:, None] * n[None, :] % ROWS).astype(np.float64) * (2 * math.pi / ROWS)
    cos, sin = np.cos(angle), np.sin(angle)
    forward = np.block([[cos, -sin], [sin, cos]])
    back = np.block([[cos, sin], [-sin, cos]]) * (2.0 / PADDED)
    inner = np.stack([*np_halves(forward), *np_halves(back)])
    outer = np.array(OUTER, dtype=np.int64)
    angle = (outer[:, None] * n[None, :]).astype(np.float64) * (2 * math.pi / PADDED)
    turn = np.stack([np.cos(angle), np.sin(angle)]).astype(np.float32)
    turn = np.ascontiguousarray(np.broadcast_to(turn[:, :, None, :], (2, KEPT, OWN, ROWS)))
    return feats, inner, turn


HALF_TURN = (3.140625, 9.67025756835937500e-4, 6.2771141529083251953e-7, 1.2154201256553420e-10)
SIN_SERIES = (1.0, -1 / 6, 1 / 120, -1 / 5040, 1 / 362880, -1 / 39916800)
COS_SERIES = (1.0, -1 / 2, 1 / 24, -1 / 720, 1 / 40320, -1 / 3628800, 1 / 479001600)


def series(coefs, x):
    total = jnp.full_like(x, coefs[-1])
    for coef in coefs[-2::-1]:
        total = total * x + coef
    return total


def sine_cosine(x):
    turns = jnp.round(x * (1 / math.pi))
    rest = x
    for part in HALF_TURN[:3]:
        rest = rest - turns * part
    half = turns * 0.5
    sign = 1.0 - 4.0 * jnp.abs(half - jnp.round(half))
    square = rest * rest
    return sign * rest * series(SIN_SERIES, square), sign * series(COS_SERIES, square)


def c_add(a, b):
    return tuple(p if q is None else q if p is None else p + q for p, q in zip(a, b))


def c_neg(a):
    return tuple(None if p is None else -p for p in a)


def c_sub(a, b):
    return tuple(
        p if q is None else -q if p is None else p - q for p, q in zip(a, b)
    )


def c_turn(a, number, count):
    number = number % count
    if number == 0:
        return a
    if 2 * number == count:
        return c_neg(a)
    re, im = a
    if 4 * number == count:
        return (None if im is None else -im, re)
    if 4 * number == 3 * count:
        return (im, None if re is None else -re)
    cos, sin = math.cos(2 * math.pi * number / count), math.sin(2 * math.pi * number / count)
    if im is None:
        return (re * cos, re * sin)
    if 8 * number == count:
        return ((re - im) * ROOT_HALF, (re + im) * ROOT_HALF)
    if 8 * number == 7 * count:
        return ((re + im) * ROOT_HALF, (im - re) * ROOT_HALF)
    if 8 * number == 3 * count:
        return ((re + im) * -ROOT_HALF, (re - im) * ROOT_HALF)
    if 8 * number == 5 * count:
        return ((im - re) * ROOT_HALF, (re + im) * -ROOT_HALF)
    return (re * cos - im * sin, re * sin + im * cos)


def transform(values, sign):
    count = len(values)
    if count == 1:
        return list(values)
    even, odd = transform(values[::2], sign), transform(values[1::2], sign)
    odd = [c_turn(v, sign * k, count) for k, v in enumerate(odd)]
    return [c_add(a, b) for a, b in zip(even, odd)] + [c_sub(a, b) for a, b in zip(even, odd)]


def outer_forward(x):
    parts = [[None] * 8 for _ in range(5)]
    for b in range(8):
        x0, x1, x2, x3 = x[b], x[8 + b], x[16 + b], x[24 + b]
        plus, minus, other, differ = x0 + x2, x0 - x2, x1 + x3, x1 - x3
        part, whole = differ * ROOT_HALF, other * ROOT_HALF
        parts[0][b] = (plus + other, None)
        parts[4][b] = (plus - other, None)
        parts[2][b] = (minus, -differ)
        parts[1][b] = (x0 + part, -(x2 + whole))
        parts[3][b] = (x0 - part, x2 - whole)
    found = {}
    for f in range(5):
        turned = [c_turn(v, -b * f, 64) for b, v in enumerate(parts[f])]
        for m, v in enumerate(transform(turned, -1)):
            found[f + 8 * m] = v
    return [found[k] for k in OUTER]


def outer_back(z):
    z = {k: z[n] for n, k in enumerate(OUTER)}
    s = ROOT_HALF
    ends, sides = z[0][0] + z[32][0], z[0][0] - z[32][0]
    (r1, i1), (r2, i2), (r3, i3) = z[8], z[16], z[24]
    one, two = s * ((r1 - i1) - (r3 + i3)), s * ((r3 - i3) - (r1 + i1))
    rsum, idiff = r1 + r3, i3 - i1
    v0 = [
        ends + r2 + rsum,
        sides - i2 + one,
        ends - r2 + idiff,
        sides + i2 + two,
        ends + r2 - rsum,
        sides - i2 - one,
        ends - r2 - idiff,
        sides + i2 - two,
    ]
    quarter = [z[4 + 8 * m] for m in range(4)]
    even = transform(quarter, 1)
    odd = transform([c_turn(v, m, 8) for m, v in enumerate(quarter)], 1)
    v4 = []
    for b in range(8):
        re, im = (odd if b % 2 else even)[b // 2]
        angle = 2 * math.pi * b / 16
        v4.append(re if b == 0 else re * math.cos(angle) - im * math.sin(angle))
    v1, v2, v3 = (
        [c_turn(v, b * f, 64) for b, v in enumerate(transform([z[f + 8 * m] for m in range(8)], 1))]
        for f in (1, 2, 3)
    )
    y = [None] * BLOCKS
    for b in range(8):
        (r1, i1), (r2, i2), (r3, i3) = v1[b], v2[b], v3[b]
        ends, sides = v0[b] + v4[b], v0[b] - v4[b]
        y[b] = ends + r2 + (r1 + r3)
        y[8 + b] = sides - i2 + s * ((r1 - i1) - (r3 + i3))
        y[16 + b] = ends - r2 + (i3 - i1)
        y[24 + b] = sides + i2 + s * ((r3 - i3) - (r1 + i1))
    return y


def spread(load, turn, spec):
    for n, (re, im) in enumerate(outer_forward([load(b) for b in range(BLOCKS)])):
        cos, sin = turn[0, n], turn[1, n]
        spec[n, :, :ROWS] = re * cos if im is None else re * cos + im * sin
        spec[n, :, ROWS:] = -(re * sin) if im is None else im * cos - re * sin


def gather(spec, turn):
    z = []
    for n, k in enumerate(OUTER):
        re, im, cos, sin = spec[n, :, :ROWS], spec[n, :, ROWS:], turn[0, n], turn[1, n]
        re, im = re * cos - im * sin, im * cos + re * sin
        z.append((re * 0.5, im * 0.5) if k in (0, 32) else (re, im))
    return outer_back(z)


def inner_pass(x, high, low):
    x_high, x_low = halves(x)
    return dot(x_high, high) + dot(x_low, high) + dot(x_high, low)


def inner_forward(spec, inner):
    x = spec[...].reshape(KEPT * OWN, 2 * ROWS)
    spec[...] = inner_pass(x, inner[0], inner[1]).reshape(KEPT, OWN, 2 * ROWS)


def inner_back(left, right, spec, inner):
    lr, li = left[:, :, :ROWS], left[:, :, ROWS:]
    rr, ri = right[:, :, :ROWS], right[:, :, ROWS:]
    re = (lr * rr + li * ri).reshape(KEPT * OWN, ROWS)
    im = (li * rr - lr * ri).reshape(KEPT * OWN, ROWS)
    x = jnp.concatenate([re, im], axis=1)
    spec[...] = inner_pass(x, inner[2], inner[3]).reshape(KEPT, OWN, 2 * ROWS)


def kernel(
    u_in, g_in, ew_in, fw_in, rate_in, gain_in, feats_in, inner_in, turn_in,
    sig_out, fgrad_out, egrad_out,
    u, g, ew, fw, rate_row, gain_row, feats, inner, turn,
    send_x, recv_x, own_par, pre, active, slopes, base, filt, decays,
    spec_f, spec_u, spec_g, spec_y, bg, q,
    send_s, recv_s, send_f, recv_f, part1, recv1, part2, recv2,
    in_sem, send_sem, recv_sem, ready,
):
    me, group = lax.axis_index("seq"), lax.axis_index("ch")
    core, y_low, x = lax.rem(me, CORES), lax.rem(lax.div(me, CORES), RUN), lax.div(me, CORES * RUN)
    z, y_high = lax.rem(group, RING), lax.div(group, RING)
    y, place = y_high * RUN + y_low, x * CORES + core

    steps = (4, 5, 3, 6, 2, 7, 1, 0)
    there = {n: lax.rem(place + n, PLACES) for n in steps}
    first = {n: lax.div(p, CORES) * (CORES * RUN) + lax.rem(p, CORES) for n, p in there.items()}

    def other_blocks(body):
        rows = (RUN - 1 - y_low, lax.rem(y_low + 2, RUN), y_low + 1 - 2 * lax.rem(y_low, 2), y_low)
        for number, row in enumerate(rows):
            for n in steps:
                if n or number < RUN - 1:
                    seq = first[n] + CORES * row
                    body(seq, {"seq": seq})

    def others_along(own, order, device_of, body):
        for index in order:
            for n in steps[:-1]:
                body(there[n], device_of(n, index))

            @pl.when(own != index)
            def _():
                body(place, device_of(0, index))

    def other_y(body):
        def device(n, index):
            return {"seq": first[n] + CORES * (index % RUN), "ch": index // RUN * RING + z}

        others_along(y, (0, 1, 7, 2, 6, 3, 5, 4), device, body)

    def other_z(body):
        def device(n, index):
            return {"seq": first[n] + CORES * y_low, "ch": y_high * RING + index}

        others_along(z, range(RING), device, body)

    barrier = pltpu.get_barrier_semaphore()
    relays = [{"ch": (1 - y_high) * RING + z}]
    relays += [{"ch": y_high * RING + lax.rem(z + n, RING)} for n in (4, 3, 5, 2, 6, 1, 7)]

    other_blocks(lambda _, device: pl.semaphore_signal(barrier, inc=1, device_id=device))
    for device in relays:
        pl.semaphore_signal(barrier, inc=1, device_id=device)

    pairs = (
        (u_in, u), (g_in, g), (ew_in, ew), (fw_in, fw), (rate_in, rate_row), (gain_in, gain_row),
        (feats_in, feats), (inner_in, inner), (turn_in, turn),
    )
    loads = [pltpu.make_async_copy(a, b, in_sem.at[n]) for n, (a, b) in enumerate(pairs)]
    for load in loads:
        load.start()

    def send(n, others, own, source, target):
        def one(there, device):
            pltpu.make_async_remote_copy(
                src_ref=source(there),
                dst_ref=target.at[own],
                send_sem=send_sem.at[n],
                recv_sem=recv_sem.at[n],
                device_id=device,
            ).start()

        others(one)

    def wait(sem, n, ref, count):
        part = ref.at[pl.ds(0, count)]
        pltpu.make_async_copy(part, part, sem.at[n]).wait()

    loads[0].wait()
    loads[1].wait()
    send_x[...] = jnp.concatenate(
        [x[...].astype(F32).T.reshape(BLOCKS, OWN, ROWS) for x in (u, g)], axis=1
    ).astype(BF16)
    pl.semaphore_wait(barrier, BLOCKS - 1 + len(relays))
    send(0, other_blocks, me, lambda there: send_x.at[there], recv_x)
    recv_x[pl.ds(me, 1)] = send_x[pl.ds(me, 1)]
    for device in relays:
        pl.semaphore_signal(ready, inc=1, device_id=device)

    for load in loads[2:]:
        load.wait()
    own_par[:, :HID] = fw[...].T
    own_par[:, HID : HID + 8] = jnp.broadcast_to(rate_row[...], (8, BLOCKS * OWN)).T
    own_par[:, HID + 8 : HID + 16] = jnp.broadcast_to(gain_row[...], (8, BLOCKS * OWN)).T
    par = own_par[pl.ds(pl.multiple_of(me * OWN, OWN), OWN), :]
    weight = par[:, :HID]
    rate = jnp.broadcast_to(par[:, HID : HID + 1], (OWN, ROWS))
    gain = jnp.broadcast_to(par[:, HID + 8 : HID + 9], (OWN, ROWS))
    w_high, w_low = halves(weight)

    e_high, e_low = halves(ew[...].T)
    pre[...] = dot(jnp.concatenate([e_high, e_high, e_low], axis=1), feats[...])

    @pl.loop(0, LENGTH // 256)
    def _(n):
        columns = pl.ds(pl.multiple_of(n * 256, 256), 256)
        sine, cosine = sine_cosine(pre[:, columns])
        high, low = halves(sine)
        active[:HID, columns] = high
        active[HID:, columns] = low
        slopes[:, columns] = cosine

    stacked = jnp.concatenate(
        [
            jnp.concatenate([w_high.astype(F32), w_high.astype(F32)], axis=1),
            jnp.concatenate([w_low.astype(F32), jnp.zeros((OWN, HID), F32)], axis=1),
        ],
        axis=0,
    ).astype(BF16)
    base[...] = dot(stacked, active[...])

    lanes = lax.broadcasted_iota(jnp.int32, (OWN, ROWS), 1)
    for b in range(BLOCKS):
        columns = slice(b * ROWS, (b + 1) * ROWS)
        decay = jnp.exp(-rate * (lanes + b * ROWS).astype(F32) / LENGTH)
        decays[b] = decay
        value = (base[:OWN, columns] + base[OWN:, columns]) * decay
        filt[b] = value.astype(BF16).astype(F32)
    spread(lambda b: filt[b], turn, spec_f)
    inner_forward(spec_f, inner)

    wait(recv_sem, 0, recv_x, BLOCKS - 1)
    spread(lambda b: recv_x[b].astype(F32)[:OWN], turn, spec_u)
    spread(lambda b: recv_x[b].astype(F32)[OWN:], turn, spec_g)
    inner_forward(spec_u, inner)
    inner_forward(spec_g, inner)

    inner_back(spec_g, spec_u, spec_y, inner)
    for b, lag in enumerate(gather(spec_y, turn)):
        bg[:, b * ROWS : (b + 1) * ROWS] = lag * decays[b]
    b_high, b_low = halves(bg[...])
    left = jnp.concatenate([w_high, w_low, w_high], axis=0)
    right = jnp.concatenate([b_high, b_high, b_low], axis=0)
    q_high, q_low = halves(dot(left, right, ((0,), (0,))) * slopes[...])
    q[:HID] = q_high
    q[HID:] = q_low
    parts = dot(feats[: 2 * EMB], q[...], ((1,), (1,)))
    embed = parts[:EMB, :HID] + parts[:EMB, HID:] + parts[EMB:, :HID]
    packed = jnp.concatenate([embed[: EMB // 2], embed[EMB // 2 :]], axis=1)
    for n in range(PLACES):
        part1[n] = packed[2 * n : 2 * n + 2]
    pl.semaphore_wait(ready, len(relays))
    slot = y * PLACES + place
    send(1, other_y, slot, lambda there: part1.at[there], recv1)
    recv1[pl.ds(slot, 1)] = part1[pl.ds(place, 1)]

    inner_back(spec_g, spec_f, spec_y, inner)
    for b, conv in enumerate(gather(spec_y, turn)):
        send_s[b] = (conv + gain * recv_x[b].astype(F32)[OWN:]).astype(BF16)
    send(2, other_blocks, me, lambda there: send_s.at[there], recv_s)
    recv_s[pl.ds(me, 1)] = send_s[pl.ds(me, 1)]

    parts = dot(jnp.concatenate([b_high, b_low], axis=0), active[...], ((1,), (1,)))
    fgrad = (parts[:OWN, :HID] + parts[:OWN, HID:] + parts[OWN:, :HID]) * (1.0 / LENGTH)
    send_f[0] = jnp.concatenate([fgrad[: OWN // 2], fgrad[OWN // 2 :]], axis=1)
    send(4, other_blocks, me, lambda there: send_f.at[0], recv_f)
    recv_f[pl.ds(me, 1)] = send_f[...]

    wait(recv_sem, 1, recv1, RING * PLACES - 1)
    part2[...] = jnp.sum(recv1[...], axis=0, keepdims=True) * (1.0 / math.sqrt(LENGTH))
    slot = place * RING + z
    send(3, other_z, slot, lambda there: part2.at[0], recv2)
    recv2[pl.ds(slot, 1)] = part2[...]

    wait(recv_sem, 2, recv_s, BLOCKS - 1)
    sig_out[...] = recv_s[...].astype(F32).reshape(BLOCKS * OWN, ROWS).T.astype(BF16)

    wait(recv_sem, 4, recv_f, BLOCKS - 1)
    pieces = recv_f[...]
    fgrad_out[...] = (
        jnp.concatenate([pieces[:, :, :HID], pieces[:, :, HID:]], axis=1).reshape(BLOCKS * OWN, HID).T
    )

    wait(recv_sem, 3, recv2, RING * PLACES - 1)
    for n in range(PLACES):
        piece = jnp.sum(recv2[n * RING : (n + 1) * RING], axis=0)
        egrad_out[2 * n : 2 * n + 2] = piece[:, :HID]
        egrad_out[EMB // 2 + 2 * n : EMB // 2 + 2 * n + 2] = piece[:, HID:]

    wait(send_sem, 0, send_x, BLOCKS - 1)
    wait(send_sem, 1, recv1, RING * PLACES - 1)
    wait(send_sem, 2, send_s, BLOCKS - 1)
    wait(send_sem, 3, recv2, RING * PLACES - 1)
    wait(send_sem, 4, recv_f, BLOCKS - 1)


def hand_over(*refs):
    copies = [pltpu.make_async_copy(refs[n], refs[3 + n], refs[6].at[n]) for n in range(3)]
    for copy in copies:
        copy.start()
    for copy in copies:
        copy.wait()


def local(inputs, out_grad, embed_weight, filter_weight, decay_rate, skip_gain):
    channels = inputs.shape[1]
    feats, inner, turn = tables()
    operands = (
        inputs,
        out_grad,
        embed_weight,
        filter_weight,
        decay_rate.reshape(1, channels),
        skip_gain.reshape(1, channels),
        jnp.asarray(feats),
        jnp.asarray(inner),
        jnp.asarray(turn),
    )
    vmem = pltpu.VMEM
    results = pl.pallas_call(
        kernel,
        out_shape=(
            pltpu.VMEM((ROWS, channels), BF16),
            pltpu.VMEM((HID, channels), F32),
            pltpu.VMEM((EMB, HID), F32),
        ),
        in_specs=[pl.BlockSpec(memory_space=pltpu.HBM)] * len(operands),
        out_specs=[pl.BlockSpec(memory_space=pltpu.VMEM)] * 3,
        scratch_shapes=[vmem(x.shape, x.dtype) for x in operands]
        + [
            vmem((BLOCKS, 2 * OWN, ROWS), BF16),
            vmem((BLOCKS, 2 * OWN, ROWS), BF16),
            vmem((channels, ROWS), F32),
            vmem((HID, LENGTH), F32),
            vmem((2 * HID, LENGTH), BF16),
            vmem((HID, LENGTH), F32),
            vmem((2 * OWN, LENGTH), F32),
            vmem((BLOCKS, OWN, ROWS), F32),
            vmem((BLOCKS, OWN, ROWS), F32),
            vmem((KEPT, OWN, 2 * ROWS), F32),
            vmem((KEPT, OWN, 2 * ROWS), F32),
            vmem((KEPT, OWN, 2 * ROWS), F32),
            vmem((KEPT, OWN, 2 * ROWS), F32),
            vmem((OWN, LENGTH), F32),
            vmem((2 * HID, LENGTH), BF16),
            vmem((BLOCKS, OWN, ROWS), BF16),
            vmem((BLOCKS, OWN, ROWS), BF16),
            vmem((1, OWN // 2, ROWS), F32),
            vmem((BLOCKS, OWN // 2, ROWS), F32),
            vmem((PLACES, 2, ROWS), F32),
            vmem((RING * PLACES, 2, ROWS), F32),
            vmem((1, 2, ROWS), F32),
            vmem((RING * PLACES, 2, ROWS), F32),
            pltpu.SemaphoreType.DMA((len(operands),)),
            pltpu.SemaphoreType.DMA((5,)),
            pltpu.SemaphoreType.DMA((5,)),
            pltpu.SemaphoreType.REGULAR,
        ],
        compiler_params=pltpu.CompilerParams(
            collective_id=0, has_side_effects=True, vmem_limit_bytes=40 * 1024 * 1024
        ),
        name="hyena_backward",
    )(*(pltpu.with_memory_space_constraint(x, pltpu.HBM) for x in operands))
    return pl.pallas_call(
        hand_over,
        out_shape=[jax.ShapeDtypeStruct(x.shape, x.dtype) for x in results],
        in_specs=[pl.BlockSpec(memory_space=pltpu.VMEM)] * 3,
        out_specs=[pl.BlockSpec(memory_space=pl.ANY)] * 3,
        scratch_shapes=[pltpu.SemaphoreType.DMA((3,))],
        name="hand_over",
    )(*(pltpu.with_memory_space_constraint(x, pltpu.VMEM) for x in results))


def solution(mesh):
    return jax.shard_map(
        local,
        mesh=mesh,
        in_specs=(P("seq", "ch"), P("seq", "ch"), P(), P(None, "ch"), P("ch"), P("ch")),
        out_specs=(P("seq", "ch"), P(None, "ch"), P()),
        check_vma=False,
    )
```

```python
import functools
import math

import jax
import jax.numpy as jnp
import ml_dtypes
import numpy as np
from jax import lax
from jax.experimental import pallas as pl
from jax.experimental.pallas import tpu as pltpu
from jax.sharding import PartitionSpec as P

F32 = jnp.float32
BF16 = jnp.bfloat16
BLOCKS = 32
ROWS = 128
OWN = 8
RUN = 4
CORES = 2
PLACES = 8
RING = 8
HID = 64
EMB = 32
LENGTH = BLOCKS * ROWS
PADDED = 2 * LENGTH
ROOT_HALF = math.sqrt(0.5)
OUTER = (
    [8 * m for m in range(5)]
    + [4 + 8 * m for m in range(4)]
    + [f + 8 * m for f in (1, 2, 3) for m in range(8)]
)
KEPT = len(OUTER)
PLACE = {k: n for n, k in enumerate(OUTER)}


def dot(a, b, contract=((1,), (0,))):
    return lax.dot_general(a, b, (contract, ((), ())), preferred_element_type=F32)


def halves(x):
    high = x.astype(BF16)
    return high, (x - high.astype(F32)).astype(BF16)


def fold(x):
    while x.shape[0] > 1:
        half = x.shape[0] // 2
        x = x[:half] + x[half:]
    return x


def np_halves(x):
    high = x.astype(ml_dtypes.bfloat16)
    low = (x - high.astype(np.float64)).astype(ml_dtypes.bfloat16)
    return high, low


@functools.cache
def tables():
    t = np.arange(LENGTH, dtype=np.int64)
    e = np.arange(EMB // 2, dtype=np.int64) + 1
    angle = (e[:, None] * t[None, :] % LENGTH).astype(np.float64) * (2 * math.pi / LENGTH)
    high, low = np_halves(np.concatenate([np.sin(angle), np.cos(angle)], axis=0))
    feats = np.concatenate([high, low, high], axis=0)
    columns = np.ascontiguousarray(np.concatenate([high, low], axis=0).T)
    n = np.arange(ROWS, dtype=np.int64)
    angle = (n[:, None] * n[None, :] % ROWS).astype(np.float64) * (2 * math.pi / ROWS)
    cos, sin = np.cos(angle), np.sin(angle)
    forward = np.block([[cos, -sin], [sin, cos]])
    back = np.block([[cos, sin], [-sin, cos]]) * (2.0 / PADDED)
    inner = np.stack([*np_halves(forward), *np_halves(back)])
    outer = np.array(OUTER, dtype=np.int64)
    angle = (outer[:, None] * n[None, :]).astype(np.float64) * (2 * math.pi / PADDED)
    turn = np.stack([np.cos(angle), np.sin(angle)]).astype(np.float32)
    turn = np.ascontiguousarray(np.broadcast_to(turn[:, :, None, :], (2, KEPT, OWN, ROWS)))
    return feats, columns, inner, turn


HALF_TURN = (3.140625, 9.67025756835937500e-4, 6.2771141529083251953e-7, 1.2154201256553420e-10)
SIN_SERIES = (1.0, -1 / 6, 1 / 120, -1 / 5040, 1 / 362880, -1 / 39916800)
COS_SERIES = (1.0, -1 / 2, 1 / 24, -1 / 720, 1 / 40320, -1 / 3628800, 1 / 479001600)


def series(coefs, x):
    total = jnp.full_like(x, coefs[-1])
    for coef in coefs[-2::-1]:
        total = total * x + coef
    return total


def sine_cosine(x):
    turns = jnp.round(x * (1 / math.pi))
    rest = x
    for part in HALF_TURN[:3]:
        rest = rest - turns * part
    half = turns * 0.5
    sign = 1.0 - 4.0 * jnp.abs(half - jnp.round(half))
    square = rest * rest
    return sign * rest * series(SIN_SERIES, square), sign * series(COS_SERIES, square)


def c_add(a, b):
    return tuple(p if q is None else q if p is None else p + q for p, q in zip(a, b))


def c_neg(a):
    return tuple(None if p is None else -p for p in a)


def c_sub(a, b):
    return tuple(
        p if q is None else -q if p is None else p - q for p, q in zip(a, b)
    )


def c_turn(a, number, count):
    number = number % count
    if number == 0:
        return a
    if 2 * number == count:
        return c_neg(a)
    re, im = a
    if 4 * number == count:
        return (None if im is None else -im, re)
    if 4 * number == 3 * count:
        return (im, None if re is None else -re)
    cos, sin = math.cos(2 * math.pi * number / count), math.sin(2 * math.pi * number / count)
    if im is None:
        return (re * cos, re * sin)
    if 8 * number == count:
        return ((re - im) * ROOT_HALF, (re + im) * ROOT_HALF)
    if 8 * number == 7 * count:
        return ((re + im) * ROOT_HALF, (im - re) * ROOT_HALF)
    if 8 * number == 3 * count:
        return ((re + im) * -ROOT_HALF, (re - im) * ROOT_HALF)
    if 8 * number == 5 * count:
        return ((im - re) * ROOT_HALF, (re + im) * -ROOT_HALF)
    return (re * cos - im * sin, re * sin + im * cos)


def transform(values, sign):
    count = len(values)
    if count == 1:
        return list(values)
    even, odd = transform(values[::2], sign), transform(values[1::2], sign)
    odd = [c_turn(v, sign * k, count) for k, v in enumerate(odd)]
    return [c_add(a, b) for a, b in zip(even, odd)] + [c_sub(a, b) for a, b in zip(even, odd)]


def outer_forward(x):
    parts = [[None] * 8 for _ in range(5)]
    for b in range(8):
        x0, x1, x2, x3 = x[b], x[8 + b], x[16 + b], x[24 + b]
        plus, minus, other, differ = x0 + x2, x0 - x2, x1 + x3, x1 - x3
        part, whole = differ * ROOT_HALF, other * ROOT_HALF
        parts[0][b] = (plus + other, None)
        parts[4][b] = (plus - other, None)
        parts[2][b] = (minus, -differ)
        parts[1][b] = (x0 + part, -(x2 + whole))
        parts[3][b] = (x0 - part, x2 - whole)
    found = {}
    for f in range(5):
        turned = [c_turn(v, -b * f, 64) for b, v in enumerate(parts[f])]
        for m, v in enumerate(transform(turned, -1)):
            found[f + 8 * m] = v
    return [found[k] for k in OUTER]


def outer_back(z):
    z = {k: z[n] for n, k in enumerate(OUTER)}
    s = ROOT_HALF
    ends, sides = z[0][0] + z[32][0], z[0][0] - z[32][0]
    (r1, i1), (r2, i2), (r3, i3) = z[8], z[16], z[24]
    one, two = s * ((r1 - i1) - (r3 + i3)), s * ((r3 - i3) - (r1 + i1))
    rsum, idiff = r1 + r3, i3 - i1
    v0 = [
        ends + r2 + rsum,
        sides - i2 + one,
        ends - r2 + idiff,
        sides + i2 + two,
        ends + r2 - rsum,
        sides - i2 - one,
        ends - r2 - idiff,
        sides + i2 - two,
    ]
    quarter = [z[4 + 8 * m] for m in range(4)]
    even = transform(quarter, 1)
    odd = transform([c_turn(v, m, 8) for m, v in enumerate(quarter)], 1)
    v4 = []
    for b in range(8):
        re, im = (odd if b % 2 else even)[b // 2]
        angle = 2 * math.pi * b / 16
        v4.append(re if b == 0 else re * math.cos(angle) - im * math.sin(angle))
    v1, v2, v3 = (
        [c_turn(v, b * f, 64) for b, v in enumerate(transform([z[f + 8 * m] for m in range(8)], 1))]
        for f in (1, 2, 3)
    )
    y = [None] * BLOCKS
    for b in range(8):
        (r1, i1), (r2, i2), (r3, i3) = v1[b], v2[b], v3[b]
        ends, sides = v0[b] + v4[b], v0[b] - v4[b]
        y[b] = ends + r2 + (r1 + r3)
        y[8 + b] = sides - i2 + s * ((r1 - i1) - (r3 + i3))
        y[16 + b] = ends - r2 + (i3 - i1)
        y[24 + b] = sides + i2 + s * ((r3 - i3) - (r1 + i1))
    return y


def spread(load, turn, spec):
    for n, (re, im) in enumerate(outer_forward([load(b) for b in range(BLOCKS)])):
        cos, sin = turn[0, n], turn[1, n]
        spec[n, :, :ROWS] = re * cos if im is None else re * cos + im * sin
        spec[n, :, ROWS:] = -(re * sin) if im is None else im * cos - re * sin


def gather(spec, turn):
    z = []
    for n, k in enumerate(OUTER):
        re, im, cos, sin = spec[n, :, :ROWS], spec[n, :, ROWS:], turn[0, n], turn[1, n]
        re, im = re * cos - im * sin, im * cos + re * sin
        z.append((re * 0.5, im * 0.5) if k in (0, 32) else (re, im))
    return outer_back(z)


def inner_pass(x, high, low):
    x_high, x_low = halves(x)
    return dot(x_high, high) + dot(x_low, high) + dot(x_high, low)


def inner_forward(spec, inner):
    x = spec[...].reshape(KEPT * OWN, 2 * ROWS)
    spec[...] = inner_pass(x, inner[0], inner[1]).reshape(KEPT, OWN, 2 * ROWS)


def inner_back(left, right, spec, inner):
    lr, li = left[:, :, :ROWS], left[:, :, ROWS:]
    rr, ri = right[:, :, :ROWS], right[:, :, ROWS:]
    re = (lr * rr + li * ri).reshape(KEPT * OWN, ROWS)
    im = (li * rr - lr * ri).reshape(KEPT * OWN, ROWS)
    x = jnp.concatenate([re, im], axis=1)
    spec[...] = inner_pass(x, inner[2], inner[3]).reshape(KEPT, OWN, 2 * ROWS)


def kernel(
    u_in, g_in, ew_in, fw_in, rate_in, gain_in, feats_in, columns_in, inner_in, turn_in,
    sig_out, fgrad_out, egrad_out,
    u, g, ew, fw, rate_row, gain_row, feats, columns, inner, turn,
    send_x, recv_x, own_par, pre, active, slopes, base, filt, decays,
    spec_f, spec_u, spec_g, spec_y, bg, weights,
    send_s, recv_s, send_f, recv_f, part1, recv1, part2, recv2,
    in_sem, send_sem, recv_sem, ready,
):
    me, group = lax.axis_index("seq"), lax.axis_index("ch")
    core, y_low, x = lax.rem(me, CORES), lax.rem(lax.div(me, CORES), RUN), lax.div(me, CORES * RUN)
    z, y_high = lax.rem(group, RING), lax.div(group, RING)
    y, place = y_high * RUN + y_low, x * CORES + core

    steps = (4, 5, 3, 6, 2, 7, 1, 0)
    there = {n: lax.rem(place + n, PLACES) for n in steps}
    first = {n: lax.div(p, CORES) * (CORES * RUN) + lax.rem(p, CORES) for n, p in there.items()}

    def other_blocks(body):
        rows = (RUN - 1 - y_low, lax.rem(y_low + 2, RUN), y_low + 1 - 2 * lax.rem(y_low, 2), y_low)
        for number, row in enumerate(rows):
            for n in steps:
                if n or number < RUN - 1:
                    seq = first[n] + CORES * row
                    body(seq, {"seq": seq})

    def others_along(own, order, device_of, body):
        for index in order:
            for n in steps[:-1]:
                body(there[n], device_of(n, index))

            @pl.when(own != index)
            def _():
                body(place, device_of(0, index))

    def other_y(body):
        def device(n, index):
            return {"seq": first[n] + CORES * (index % RUN), "ch": index // RUN * RING + z}

        others_along(y, (0, 1, 7, 2, 6, 3, 5, 4), device, body)

    def other_z(body):
        def device(n, index):
            return {"seq": first[n] + CORES * y_low, "ch": y_high * RING + index}

        others_along(z, range(RING), device, body)

    barrier = pltpu.get_barrier_semaphore()

    def along_z(n):
        return {"ch": y_high * RING + lax.rem(z + n, RING)}

    second = [along_z(2), along_z(RING - 2)]
    relays = [{"ch": (1 - y_high) * RING + z}, *second, along_z(1), along_z(RING - 1)]

    other_blocks(lambda _, device: pl.semaphore_signal(barrier, inc=1, device_id=device))
    for device in relays:
        pl.semaphore_signal(barrier, inc=1, device_id=device)

    pairs = (
        (u_in, u), (g_in, g), (ew_in, ew), (fw_in, fw), (rate_in, rate_row), (gain_in, gain_row),
        (feats_in, feats), (columns_in, columns), (inner_in, inner), (turn_in, turn),
    )
    loads = [pltpu.make_async_copy(a, b, in_sem.at[n]) for n, (a, b) in enumerate(pairs)]
    for load in loads:
        load.start()

    def send(n, others, own, source, target):
        def one(there, device):
            pltpu.make_async_remote_copy(
                src_ref=source(there),
                dst_ref=target.at[own],
                send_sem=send_sem.at[n],
                recv_sem=recv_sem.at[n],
                device_id=device,
            ).start()

        others(one)

    def wait(sem, n, ref, count):
        part = ref.at[pl.ds(0, count)]
        pltpu.make_async_copy(part, part, sem.at[n]).wait()

    loads[0].wait()
    loads[1].wait()
    send_x[...] = jnp.concatenate(
        [x[...].astype(F32).T.reshape(BLOCKS, OWN, ROWS) for x in (u, g)], axis=1
    ).astype(BF16)
    pl.semaphore_wait(barrier, BLOCKS - 1 + len(relays))
    send(0, other_blocks, me, lambda there: send_x.at[there], recv_x)
    recv_x[pl.ds(me, 1)] = send_x[pl.ds(me, 1)]
    for device in relays:
        pl.semaphore_signal(ready.at[0], inc=1, device_id=device)

    for load in loads[2:]:
        load.wait()
    own_par[:, :HID] = fw[...].T
    own_par[:, HID : HID + 8] = jnp.broadcast_to(rate_row[...], (8, BLOCKS * OWN)).T
    own_par[:, HID + 8 : HID + 16] = jnp.broadcast_to(gain_row[...], (8, BLOCKS * OWN)).T
    par = own_par[pl.ds(pl.multiple_of(me * OWN, OWN), OWN), :]
    weight = par[:, :HID]
    rate = jnp.broadcast_to(par[:, HID : HID + 1], (OWN, ROWS))
    gain = jnp.broadcast_to(par[:, HID + 8 : HID + 9], (OWN, ROWS))
    w_high, w_low = halves(weight)

    e_high, e_low = halves(ew[...].T)
    pre[...] = dot(jnp.concatenate([e_high, e_high, e_low], axis=1), feats[...])

    @pl.loop(0, LENGTH // 256)
    def _(n):
        part = pl.ds(pl.multiple_of(n * 256, 256), 256)
        sine, cosine = sine_cosine(pre[:, part])
        high, low = halves(sine)
        active[:HID, part] = high
        active[HID:, part] = low
        slopes[:, part] = cosine

    stacked = jnp.concatenate(
        [
            jnp.concatenate([w_high.astype(F32), w_high.astype(F32)], axis=1),
            jnp.concatenate([w_low.astype(F32), jnp.zeros((OWN, HID), F32)], axis=1),
        ],
        axis=0,
    ).astype(BF16)
    base[...] = dot(stacked, active[...])

    w_left, w_right = w_high.astype(F32), w_low.astype(F32)
    tall = jnp.concatenate([w_left, w_left, w_right, jnp.zeros_like(w_left)], axis=0)
    weights[...] = tall.T.astype(BF16)

    lanes = lax.broadcasted_iota(jnp.int32, (OWN, ROWS), 1)
    for b in range(BLOCKS):
        part = slice(b * ROWS, (b + 1) * ROWS)
        decay = jnp.exp(-rate * (lanes + b * ROWS).astype(F32) / LENGTH)
        decays[b] = decay
        value = (base[:OWN, part] + base[OWN:, part]) * decay
        filt[b] = value.astype(BF16).astype(F32)
    spread(lambda b: filt[b], turn, spec_f)
    inner_forward(spec_f, inner)

    wait(recv_sem, 0, recv_x, BLOCKS - 1)
    spread(lambda b: recv_x[b].astype(F32)[:OWN], turn, spec_u)
    spread(lambda b: recv_x[b].astype(F32)[OWN:], turn, spec_g)
    inner_forward(spec_u, inner)
    inner_forward(spec_g, inner)

    inner_back(spec_g, spec_u, spec_y, inner)
    for b, lag in enumerate(gather(spec_y, turn)):
        grad = lag * decays[b]
        high = grad.astype(BF16).astype(F32)
        pair = jnp.concatenate([high, grad - high], axis=0).astype(BF16)
        bg[: 2 * OWN, b * ROWS : (b + 1) * ROWS] = pair
        bg[2 * OWN :, b * ROWS : (b + 1) * ROWS] = pair
    q_high, q_low = halves(dot(weights[...], bg[...]) * slopes[...])
    parts = dot(jnp.concatenate([q_high, q_low], axis=0), columns[...])
    embed = (parts[:HID, :EMB] + parts[:HID, EMB:] + parts[HID:, :EMB]).T
    packed = jnp.concatenate([embed[: EMB // 2], embed[EMB // 2 :]], axis=1)
    for n in range(PLACES):
        part1[n] = packed[2 * n : 2 * n + 2]
    pl.semaphore_wait(ready.at[0], len(relays))
    slot = y * PLACES + place
    send(1, other_y, slot, lambda there: part1.at[there], recv1)
    recv1[pl.ds(slot, 1)] = part1[pl.ds(place, 1)]
    for device in second:
        pl.semaphore_signal(ready.at[1], inc=1, device_id=device)

    inner_back(spec_g, spec_f, spec_y, inner)
    for b, conv in enumerate(gather(spec_y, turn)):
        send_s[b] = (conv + gain * recv_x[b].astype(F32)[OWN:]).astype(BF16)
    send(2, other_blocks, me, lambda there: send_s.at[there], recv_s)
    recv_s[pl.ds(me, 1)] = send_s[pl.ds(me, 1)]

    parts = dot(bg[: 2 * OWN], active[...], ((1,), (1,)))
    fgrad = (parts[:OWN, :HID] + parts[:OWN, HID:] + parts[OWN:, :HID]) * (1.0 / LENGTH)
    send_f[0] = jnp.concatenate([fgrad[: OWN // 2], fgrad[OWN // 2 :]], axis=1)
    send(4, other_blocks, me, lambda there: send_f.at[0], recv_f)
    recv_f[pl.ds(me, 1)] = send_f[...]

    wait(recv_sem, 1, recv1, RING * PLACES - 1)
    part2[...] = fold(recv1[...]) * (1.0 / math.sqrt(LENGTH))
    slot = place * RING + z
    pl.semaphore_wait(ready.at[1], len(second))
    send(3, other_z, slot, lambda there: part2.at[0], recv2)
    recv2[pl.ds(slot, 1)] = part2[...]

    wait(recv_sem, 2, recv_s, BLOCKS - 1)
    sig_out[...] = recv_s[...].astype(F32).reshape(BLOCKS * OWN, ROWS).T.astype(BF16)

    wait(recv_sem, 4, recv_f, BLOCKS - 1)
    pieces = recv_f[...]
    fgrad_out[...] = (
        jnp.concatenate([pieces[:, :, :HID], pieces[:, :, HID:]], axis=1).reshape(BLOCKS * OWN, HID).T
    )

    wait(send_sem, 0, send_x, BLOCKS - 1)
    wait(send_sem, 1, recv1, RING * PLACES - 1)
    wait(send_sem, 2, send_s, BLOCKS - 1)
    wait(send_sem, 3, recv2, RING * PLACES - 1)
    wait(send_sem, 4, recv_f, BLOCKS - 1)

    wait(recv_sem, 3, recv2, RING * PLACES - 1)
    for n in range(PLACES):
        piece = fold(recv2[n * RING : (n + 1) * RING])[0]
        egrad_out[2 * n : 2 * n + 2] = piece[:, :HID]
        egrad_out[EMB // 2 + 2 * n : EMB // 2 + 2 * n + 2] = piece[:, HID:]


def hand_over(*refs):
    copies = [pltpu.make_async_copy(refs[n], refs[3 + n], refs[6].at[n]) for n in range(3)]
    for copy in copies:
        copy.start()
    for copy in copies:
        copy.wait()


def local(inputs, out_grad, embed_weight, filter_weight, decay_rate, skip_gain):
    channels = inputs.shape[1]
    feats, columns, inner, turn = tables()
    operands = (
        inputs,
        out_grad,
        embed_weight,
        filter_weight,
        decay_rate.reshape(1, channels),
        skip_gain.reshape(1, channels),
        jnp.asarray(feats),
        jnp.asarray(columns),
        jnp.asarray(inner),
        jnp.asarray(turn),
    )
    vmem = pltpu.VMEM
    results = pl.pallas_call(
        kernel,
        out_shape=(
            pltpu.VMEM((ROWS, channels), BF16),
            pltpu.VMEM((HID, channels), F32),
            pltpu.VMEM((EMB, HID), F32),
        ),
        in_specs=[pl.BlockSpec(memory_space=pltpu.HBM)] * len(operands),
        out_specs=[pl.BlockSpec(memory_space=pltpu.VMEM)] * 3,
        scratch_shapes=[vmem(x.shape, x.dtype) for x in operands]
        + [
            vmem((BLOCKS, 2 * OWN, ROWS), BF16),
            vmem((BLOCKS, 2 * OWN, ROWS), BF16),
            vmem((channels, ROWS), F32),
            vmem((HID, LENGTH), F32),
            vmem((2 * HID, LENGTH), BF16),
            vmem((HID, LENGTH), F32),
            vmem((2 * OWN, LENGTH), F32),
            vmem((BLOCKS, OWN, ROWS), F32),
            vmem((BLOCKS, OWN, ROWS), F32),
            vmem((KEPT, OWN, 2 * ROWS), F32),
            vmem((KEPT, OWN, 2 * ROWS), F32),
            vmem((KEPT, OWN, 2 * ROWS), F32),
            vmem((KEPT, OWN, 2 * ROWS), F32),
            vmem((4 * OWN, LENGTH), BF16),
            vmem((HID, 4 * OWN), BF16),
            vmem((BLOCKS, OWN, ROWS), BF16),
            vmem((BLOCKS, OWN, ROWS), BF16),
            vmem((1, OWN // 2, ROWS), F32),
            vmem((BLOCKS, OWN // 2, ROWS), F32),
            vmem((PLACES, 2, ROWS), F32),
            vmem((RING * PLACES, 2, ROWS), F32),
            vmem((1, 2, ROWS), F32),
            vmem((RING * PLACES, 2, ROWS), F32),
            pltpu.SemaphoreType.DMA((len(operands),)),
            pltpu.SemaphoreType.DMA((5,)),
            pltpu.SemaphoreType.DMA((5,)),
            pltpu.SemaphoreType.REGULAR((2,)),
        ],
        compiler_params=pltpu.CompilerParams(
            collective_id=0, has_side_effects=True, vmem_limit_bytes=40 * 1024 * 1024
        ),
        name="hyena_backward",
    )(*(pltpu.with_memory_space_constraint(x, pltpu.HBM) for x in operands))
    return pl.pallas_call(
        hand_over,
        out_shape=[jax.ShapeDtypeStruct(x.shape, x.dtype) for x in results],
        in_specs=[pl.BlockSpec(memory_space=pltpu.VMEM)] * 3,
        out_specs=[pl.BlockSpec(memory_space=pl.ANY)] * 3,
        scratch_shapes=[pltpu.SemaphoreType.DMA((3,))],
        name="hand_over",
    )(*(pltpu.with_memory_space_constraint(x, pltpu.VMEM) for x in results))


def solution(mesh):
    return jax.shard_map(
        local,
        mesh=mesh,
        in_specs=(P("seq", "ch"), P("seq", "ch"), P(), P(None, "ch"), P("ch"), P("ch")),
        out_specs=(P("seq", "ch"), P(None, "ch"), P()),
        check_vma=False,
    )
```

```python
import functools
import math

import jax
import jax.numpy as jnp
import ml_dtypes
import numpy as np
from jax import lax
from jax.experimental import pallas as pl
from jax.experimental.pallas import tpu as pltpu
from jax.sharding import PartitionSpec as P

F32 = jnp.float32
BF16 = jnp.bfloat16
BLOCKS = 32
ROWS = 128
OWN = 8
RUN = 4
CORES = 2
PLACES = 8
RING = 8
HID = 64
EMB = 32
LENGTH = BLOCKS * ROWS
PADDED = 2 * LENGTH
ROOT_HALF = math.sqrt(0.5)
OUTER = (
    [8 * m for m in range(5)]
    + [4 + 8 * m for m in range(4)]
    + [f + 8 * m for f in (1, 2, 3) for m in range(8)]
)
KEPT = len(OUTER)
PLACE = {k: n for n, k in enumerate(OUTER)}


def dot(a, b, contract=((1,), (0,))):
    return lax.dot_general(a, b, (contract, ((), ())), preferred_element_type=F32)


def halves(x):
    high = x.astype(BF16)
    return high, (x - high.astype(F32)).astype(BF16)


def fold(x):
    while x.shape[0] > 1:
        half = x.shape[0] // 2
        x = x[:half] + x[half:]
    return x


def np_halves(x):
    high = x.astype(ml_dtypes.bfloat16)
    low = (x - high.astype(np.float64)).astype(ml_dtypes.bfloat16)
    return high, low


@functools.cache
def tables():
    t = np.arange(LENGTH, dtype=np.int64)
    e = np.arange(EMB // 2, dtype=np.int64) + 1
    angle = (e[:, None] * t[None, :] % LENGTH).astype(np.float64) * (2 * math.pi / LENGTH)
    high, low = np_halves(np.concatenate([np.sin(angle), np.cos(angle)], axis=0))
    feats = np.concatenate([high, low, high], axis=0)
    columns = np.ascontiguousarray(np.concatenate([high, low], axis=0).T)
    n = np.arange(ROWS, dtype=np.int64)
    angle = (n[:, None] * n[None, :] % ROWS).astype(np.float64) * (2 * math.pi / ROWS)
    cos, sin = np.cos(angle), np.sin(angle)
    forward = np.block([[cos, -sin], [sin, cos]])
    back = np.block([[cos, sin], [-sin, cos]]) * (2.0 / PADDED)
    inner = np.stack([*np_halves(forward), *np_halves(back)])
    outer = np.array(OUTER, dtype=np.int64)
    angle = (outer[:, None] * n[None, :]).astype(np.float64) * (2 * math.pi / PADDED)
    turn = np.stack([np.cos(angle), np.sin(angle)]).astype(np.float32)
    turn = np.ascontiguousarray(np.broadcast_to(turn[:, :, None, :], (2, KEPT, OWN, ROWS)))
    return feats, columns, inner, turn


HALF_TURN = (3.140625, 9.67025756835937500e-4, 6.2771141529083251953e-7, 1.2154201256553420e-10)
SIN_SERIES = (1.0, -1 / 6, 1 / 120, -1 / 5040, 1 / 362880, -1 / 39916800)
COS_SERIES = (1.0, -1 / 2, 1 / 24, -1 / 720, 1 / 40320, -1 / 3628800, 1 / 479001600)


def series(coefs, x):
    total = jnp.full_like(x, coefs[-1])
    for coef in coefs[-2::-1]:
        total = total * x + coef
    return total


def sine_cosine(x):
    turns = jnp.round(x * (1 / math.pi))
    rest = x
    for part in HALF_TURN[:3]:
        rest = rest - turns * part
    half = turns * 0.5
    sign = 1.0 - 4.0 * jnp.abs(half - jnp.round(half))
    square = rest * rest
    return sign * rest * series(SIN_SERIES, square), sign * series(COS_SERIES, square)


def c_add(a, b):
    return tuple(p if q is None else q if p is None else p + q for p, q in zip(a, b))


def c_neg(a):
    return tuple(None if p is None else -p for p in a)


def c_sub(a, b):
    return tuple(
        p if q is None else -q if p is None else p - q for p, q in zip(a, b)
    )


def c_turn(a, number, count):
    number = number % count
    if number == 0:
        return a
    if 2 * number == count:
        return c_neg(a)
    re, im = a
    if 4 * number == count:
        return (None if im is None else -im, re)
    if 4 * number == 3 * count:
        return (im, None if re is None else -re)
    cos, sin = math.cos(2 * math.pi * number / count), math.sin(2 * math.pi * number / count)
    if im is None:
        return (re * cos, re * sin)
    if 8 * number == count:
        return ((re - im) * ROOT_HALF, (re + im) * ROOT_HALF)
    if 8 * number == 7 * count:
        return ((re + im) * ROOT_HALF, (im - re) * ROOT_HALF)
    if 8 * number == 3 * count:
        return ((re + im) * -ROOT_HALF, (re - im) * ROOT_HALF)
    if 8 * number == 5 * count:
        return ((im - re) * ROOT_HALF, (re + im) * -ROOT_HALF)
    return (re * cos - im * sin, re * sin + im * cos)


def transform(values, sign):
    count = len(values)
    if count == 1:
        return list(values)
    even, odd = transform(values[::2], sign), transform(values[1::2], sign)
    odd = [c_turn(v, sign * k, count) for k, v in enumerate(odd)]
    return [c_add(a, b) for a, b in zip(even, odd)] + [c_sub(a, b) for a, b in zip(even, odd)]


def outer_forward(x):
    parts = [[None] * 8 for _ in range(5)]
    for b in range(8):
        x0, x1, x2, x3 = x[b], x[8 + b], x[16 + b], x[24 + b]
        plus, minus, other, differ = x0 + x2, x0 - x2, x1 + x3, x1 - x3
        part, whole = differ * ROOT_HALF, other * ROOT_HALF
        parts[0][b] = (plus + other, None)
        parts[4][b] = (plus - other, None)
        parts[2][b] = (minus, -differ)
        parts[1][b] = (x0 + part, -(x2 + whole))
        parts[3][b] = (x0 - part, x2 - whole)
    found = {}
    for f in range(5):
        turned = [c_turn(v, -b * f, 64) for b, v in enumerate(parts[f])]
        for m, v in enumerate(transform(turned, -1)):
            found[f + 8 * m] = v
    return [found[k] for k in OUTER]


def outer_back(z):
    z = {k: z[n] for n, k in enumerate(OUTER)}
    s = ROOT_HALF
    ends, sides = z[0][0] + z[32][0], z[0][0] - z[32][0]
    (r1, i1), (r2, i2), (r3, i3) = z[8], z[16], z[24]
    one, two = s * ((r1 - i1) - (r3 + i3)), s * ((r3 - i3) - (r1 + i1))
    rsum, idiff = r1 + r3, i3 - i1
    v0 = [
        ends + r2 + rsum,
        sides - i2 + one,
        ends - r2 + idiff,
        sides + i2 + two,
        ends + r2 - rsum,
        sides - i2 - one,
        ends - r2 - idiff,
        sides + i2 - two,
    ]
    quarter = [z[4 + 8 * m] for m in range(4)]
    even = transform(quarter, 1)
    odd = transform([c_turn(v, m, 8) for m, v in enumerate(quarter)], 1)
    v4 = []
    for b in range(8):
        re, im = (odd if b % 2 else even)[b // 2]
        angle = 2 * math.pi * b / 16
        v4.append(re if b == 0 else re * math.cos(angle) - im * math.sin(angle))
    v1, v2, v3 = (
        [c_turn(v, b * f, 64) for b, v in enumerate(transform([z[f + 8 * m] for m in range(8)], 1))]
        for f in (1, 2, 3)
    )
    y = [None] * BLOCKS
    for b in range(8):
        (r1, i1), (r2, i2), (r3, i3) = v1[b], v2[b], v3[b]
        ends, sides = v0[b] + v4[b], v0[b] - v4[b]
        y[b] = ends + r2 + (r1 + r3)
        y[8 + b] = sides - i2 + s * ((r1 - i1) - (r3 + i3))
        y[16 + b] = ends - r2 + (i3 - i1)
        y[24 + b] = sides + i2 + s * ((r3 - i3) - (r1 + i1))
    return y


def spread(load, turn, spec):
    for n, (re, im) in enumerate(outer_forward([load(b) for b in range(BLOCKS)])):
        cos, sin = turn[0, n], turn[1, n]
        spec[n, :, :ROWS] = re * cos if im is None else re * cos + im * sin
        spec[n, :, ROWS:] = -(re * sin) if im is None else im * cos - re * sin


def gather(spec, turn):
    z = []
    for n, k in enumerate(OUTER):
        re, im, cos, sin = spec[n, :, :ROWS], spec[n, :, ROWS:], turn[0, n], turn[1, n]
        re, im = re * cos - im * sin, im * cos + re * sin
        z.append((re * 0.5, im * 0.5) if k in (0, 32) else (re, im))
    return outer_back(z)


def inner_pass(x, high, low):
    x_high, x_low = halves(x)
    return dot(x_high, high) + dot(x_low, high) + dot(x_high, low)


def inner_forward(spec, inner):
    x = spec[...].reshape(KEPT * OWN, 2 * ROWS)
    spec[...] = inner_pass(x, inner[0], inner[1]).reshape(KEPT, OWN, 2 * ROWS)


def inner_back(left, right, spec, inner):
    lr, li = left[:, :, :ROWS], left[:, :, ROWS:]
    rr, ri = right[:, :, :ROWS], right[:, :, ROWS:]
    re = (lr * rr + li * ri).reshape(KEPT * OWN, ROWS)
    im = (li * rr - lr * ri).reshape(KEPT * OWN, ROWS)
    x = jnp.concatenate([re, im], axis=1)
    spec[...] = inner_pass(x, inner[2], inner[3]).reshape(KEPT, OWN, 2 * ROWS)


def kernel(
    u_in, g_in, ew_in, fw_in, rate_in, gain_in, feats_in, columns_in, inner_in, turn_in,
    sig_out, fgrad_out, egrad_out,
    u, g, ew, fw, rate_row, gain_row, feats, columns, inner, turn,
    send_u, recv_u, send_g, recv_g, own_par, pre, active, slopes, base, filt, decays,
    spec_f, spec_u, spec_g, spec_y, bg, weights,
    send_s, recv_s, send_f, recv_f, part1, recv1, part2, recv2,
    in_sem, send_sem, recv_sem, ready,
):
    me, group = lax.axis_index("seq"), lax.axis_index("ch")
    core, y_low, x = lax.rem(me, CORES), lax.rem(lax.div(me, CORES), RUN), lax.div(me, CORES * RUN)
    z, y_high = lax.rem(group, RING), lax.div(group, RING)
    y, place = y_high * RUN + y_low, x * CORES + core

    steps = (4, 5, 3, 6, 2, 7, 1, 0)
    there = {n: lax.rem(place + n, PLACES) for n in steps}
    first = {n: lax.div(p, CORES) * (CORES * RUN) + lax.rem(p, CORES) for n, p in there.items()}

    def other_blocks(*bodies):
        rows = [lax.select(y_low == 0, RUN - 1 - n, n + (n >= y_low).astype(jnp.int32)) for n in range(RUN - 1)]
        rows.append(y_low)
        for number, row in enumerate(rows):
            seqs = [first[n] + CORES * row for n in steps if n or number < RUN - 1]
            for one in bodies:
                for seq in seqs:
                    one(seq, {"seq": seq})

    def others_along(own, order, device_of, body):
        for index in order:
            for n in steps[:-1]:
                body(there[n], device_of(n, index))

            @pl.when(own != index)
            def _():
                body(place, device_of(0, index))

    def other_y(body):
        def device(n, index):
            return {"seq": first[n] + CORES * (index % RUN), "ch": index // RUN * RING + z}

        others_along(y, (0, 1, 7, 2, 6, 3, 5, 4), device, body)

    def other_z(body):
        def device(n, index):
            return {"seq": first[n] + CORES * y_low, "ch": y_high * RING + index}

        others_along(z, range(RING), device, body)

    barrier = pltpu.get_barrier_semaphore()

    def along_z(n):
        return {"ch": y_high * RING + lax.rem(z + n, RING)}

    second = [along_z(2), along_z(RING - 2)]
    relays = [{"ch": (1 - y_high) * RING + z}, *second, along_z(1), along_z(RING - 1)]

    other_blocks(lambda _, device: pl.semaphore_signal(barrier, inc=1, device_id=device))
    for device in relays:
        pl.semaphore_signal(barrier, inc=1, device_id=device)

    pairs = (
        (u_in, u), (g_in, g), (ew_in, ew), (fw_in, fw), (rate_in, rate_row), (gain_in, gain_row),
        (feats_in, feats), (columns_in, columns), (inner_in, inner), (turn_in, turn),
    )
    loads = [pltpu.make_async_copy(a, b, in_sem.at[n]) for n, (a, b) in enumerate(pairs)]
    for load in loads:
        load.start()

    def send(n, others, own, source, target):
        others(sender(n, own, source, target))

    def sender(n, own, source, target):
        def one(there, device):
            pltpu.make_async_remote_copy(
                src_ref=source(there),
                dst_ref=target.at[own],
                send_sem=send_sem.at[n],
                recv_sem=recv_sem.at[n],
                device_id=device,
            ).start()

        return one

    def wait(sem, n, ref, count):
        part = ref.at[pl.ds(0, count)]
        pltpu.make_async_copy(part, part, sem.at[n]).wait()

    loads[0].wait()
    loads[1].wait()
    for x_ref, send_ref in ((u, send_u), (g, send_g)):
        send_ref[...] = x_ref[...].astype(F32).T.reshape(BLOCKS, OWN, ROWS).astype(BF16)
    pl.semaphore_wait(barrier, BLOCKS - 1 + len(relays))
    other_blocks(
        sender(0, me, lambda there: send_u.at[there], recv_u),
        sender(5, me, lambda there: send_g.at[there], recv_g),
    )
    recv_u[pl.ds(me, 1)] = send_u[pl.ds(me, 1)]
    recv_g[pl.ds(me, 1)] = send_g[pl.ds(me, 1)]
    for device in relays:
        pl.semaphore_signal(ready.at[0], inc=1, device_id=device)

    for load in loads[2:]:
        load.wait()
    own_par[:, :HID] = fw[...].T
    own_par[:, HID : HID + 8] = jnp.broadcast_to(rate_row[...], (8, BLOCKS * OWN)).T
    own_par[:, HID + 8 : HID + 16] = jnp.broadcast_to(gain_row[...], (8, BLOCKS * OWN)).T
    par = own_par[pl.ds(pl.multiple_of(me * OWN, OWN), OWN), :]
    weight = par[:, :HID]
    rate = jnp.broadcast_to(par[:, HID : HID + 1], (OWN, ROWS))
    gain = jnp.broadcast_to(par[:, HID + 8 : HID + 9], (OWN, ROWS))
    w_high, w_low = halves(weight)

    e_high, e_low = halves(ew[...].T)
    pre[...] = dot(jnp.concatenate([e_high, e_high, e_low], axis=1), feats[...])

    @pl.loop(0, LENGTH // 256)
    def _(n):
        part = pl.ds(pl.multiple_of(n * 256, 256), 256)
        sine, cosine = sine_cosine(pre[:, part])
        high, low = halves(sine)
        active[:HID, part] = high
        active[HID:, part] = low
        slopes[:, part] = cosine

    stacked = jnp.concatenate(
        [
            jnp.concatenate([w_high.astype(F32), w_high.astype(F32)], axis=1),
            jnp.concatenate([w_low.astype(F32), jnp.zeros((OWN, HID), F32)], axis=1),
        ],
        axis=0,
    ).astype(BF16)
    base[...] = dot(stacked, active[...])

    w_left, w_right = w_high.astype(F32), w_low.astype(F32)
    tall = jnp.concatenate([w_left, w_left, w_right, jnp.zeros_like(w_left)], axis=0)
    weights[...] = tall.T.astype(BF16)

    lanes = lax.broadcasted_iota(jnp.int32, (OWN, ROWS), 1)
    for b in range(BLOCKS):
        part = slice(b * ROWS, (b + 1) * ROWS)
        decay = jnp.exp(-rate * (lanes + b * ROWS).astype(F32) / LENGTH)
        decays[b] = decay
        value = (base[:OWN, part] + base[OWN:, part]) * decay
        filt[b] = value.astype(BF16).astype(F32)
    spread(lambda b: filt[b], turn, spec_f)
    inner_forward(spec_f, inner)

    wait(recv_sem, 0, recv_u, BLOCKS - 1)
    spread(lambda b: recv_u[b].astype(F32), turn, spec_u)
    inner_forward(spec_u, inner)
    wait(recv_sem, 5, recv_g, BLOCKS - 1)
    spread(lambda b: recv_g[b].astype(F32), turn, spec_g)
    inner_forward(spec_g, inner)

    inner_back(spec_g, spec_u, spec_y, inner)
    for b, lag in enumerate(gather(spec_y, turn)):
        grad = lag * decays[b]
        high = grad.astype(BF16).astype(F32)
        pair = jnp.concatenate([high, grad - high], axis=0).astype(BF16)
        bg[: 2 * OWN, b * ROWS : (b + 1) * ROWS] = pair
        bg[2 * OWN :, b * ROWS : (b + 1) * ROWS] = pair
    q_high, q_low = halves(dot(weights[...], bg[...]) * slopes[...])
    parts = dot(jnp.concatenate([q_high, q_low], axis=0), columns[...])
    embed = (parts[:HID, :EMB] + parts[:HID, EMB:] + parts[HID:, :EMB]).T
    packed = jnp.concatenate([embed[: EMB // 2], embed[EMB // 2 :]], axis=1)
    for n in range(PLACES):
        part1[n] = packed[2 * n : 2 * n + 2]
    pl.semaphore_wait(ready.at[0], len(relays))
    slot = y * PLACES + place
    send(1, other_y, slot, lambda there: part1.at[there], recv1)
    recv1[pl.ds(slot, 1)] = part1[pl.ds(place, 1)]
    for device in second:
        pl.semaphore_signal(ready.at[1], inc=1, device_id=device)

    inner_back(spec_g, spec_f, spec_y, inner)
    for b, conv in enumerate(gather(spec_y, turn)):
        send_s[b] = (conv + gain * recv_g[b].astype(F32)).astype(BF16)
    send(2, other_blocks, me, lambda there: send_s.at[there], recv_s)
    recv_s[pl.ds(me, 1)] = send_s[pl.ds(me, 1)]

    parts = dot(bg[: 2 * OWN], active[...], ((1,), (1,)))
    fgrad = (parts[:OWN, :HID] + parts[:OWN, HID:] + parts[OWN:, :HID]) * (1.0 / LENGTH)
    send_f[0] = jnp.concatenate([fgrad[: OWN // 2], fgrad[OWN // 2 :]], axis=1)
    send(4, other_blocks, me, lambda there: send_f.at[0], recv_f)
    recv_f[pl.ds(me, 1)] = send_f[...]

    wait(recv_sem, 1, recv1, RING * PLACES - 1)
    part2[...] = fold(recv1[...]) * (1.0 / math.sqrt(LENGTH))
    slot = place * RING + z
    pl.semaphore_wait(ready.at[1], len(second))
    send(3, other_z, slot, lambda there: part2.at[0], recv2)
    recv2[pl.ds(slot, 1)] = part2[...]

    wait(recv_sem, 2, recv_s, BLOCKS - 1)
    sig_out[...] = recv_s[...].astype(F32).reshape(BLOCKS * OWN, ROWS).T.astype(BF16)

    wait(recv_sem, 4, recv_f, BLOCKS - 1)
    pieces = recv_f[...]
    fgrad_out[...] = (
        jnp.concatenate([pieces[:, :, :HID], pieces[:, :, HID:]], axis=1).reshape(BLOCKS * OWN, HID).T
    )

    wait(send_sem, 0, send_u, BLOCKS - 1)
    wait(send_sem, 5, send_g, BLOCKS - 1)
    wait(send_sem, 1, recv1, RING * PLACES - 1)
    wait(send_sem, 2, send_s, BLOCKS - 1)
    wait(send_sem, 3, recv2, RING * PLACES - 1)
    wait(send_sem, 4, recv_f, BLOCKS - 1)

    wait(recv_sem, 3, recv2, RING * PLACES - 1)
    for n in range(PLACES):
        piece = fold(recv2[n * RING : (n + 1) * RING])[0]
        egrad_out[2 * n : 2 * n + 2] = piece[:, :HID]
        egrad_out[EMB // 2 + 2 * n : EMB // 2 + 2 * n + 2] = piece[:, HID:]


def hand_over(*refs):
    copies = [pltpu.make_async_copy(refs[n], refs[3 + n], refs[6].at[n]) for n in range(3)]
    for copy in copies:
        copy.start()
    for copy in copies:
        copy.wait()


def local(inputs, out_grad, embed_weight, filter_weight, decay_rate, skip_gain):
    channels = inputs.shape[1]
    feats, columns, inner, turn = tables()
    operands = (
        inputs,
        out_grad,
        embed_weight,
        filter_weight,
        decay_rate.reshape(1, channels),
        skip_gain.reshape(1, channels),
        jnp.asarray(feats),
        jnp.asarray(columns),
        jnp.asarray(inner),
        jnp.asarray(turn),
    )
    vmem = pltpu.VMEM
    results = pl.pallas_call(
        kernel,
        out_shape=(
            pltpu.VMEM((ROWS, channels), BF16),
            pltpu.VMEM((HID, channels), F32),
            pltpu.VMEM((EMB, HID), F32),
        ),
        in_specs=[pl.BlockSpec(memory_space=pltpu.HBM)] * len(operands),
        out_specs=[pl.BlockSpec(memory_space=pltpu.VMEM)] * 3,
        scratch_shapes=[vmem(x.shape, x.dtype) for x in operands]
        + [
            vmem((BLOCKS, OWN, ROWS), BF16),
            vmem((BLOCKS, OWN, ROWS), BF16),
            vmem((BLOCKS, OWN, ROWS), BF16),
            vmem((BLOCKS, OWN, ROWS), BF16),
            vmem((channels, ROWS), F32),
            vmem((HID, LENGTH), F32),
            vmem((2 * HID, LENGTH), BF16),
            vmem((HID, LENGTH), F32),
            vmem((2 * OWN, LENGTH), F32),
            vmem((BLOCKS, OWN, ROWS), F32),
            vmem((BLOCKS, OWN, ROWS), F32),
            vmem((KEPT, OWN, 2 * ROWS), F32),
            vmem((KEPT, OWN, 2 * ROWS), F32),
            vmem((KEPT, OWN, 2 * ROWS), F32),
            vmem((KEPT, OWN, 2 * ROWS), F32),
            vmem((4 * OWN, LENGTH), BF16),
            vmem((HID, 4 * OWN), BF16),
            vmem((BLOCKS, OWN, ROWS), BF16),
            vmem((BLOCKS, OWN, ROWS), BF16),
            vmem((1, OWN // 2, ROWS), F32),
            vmem((BLOCKS, OWN // 2, ROWS), F32),
            vmem((PLACES, 2, ROWS), F32),
            vmem((RING * PLACES, 2, ROWS), F32),
            vmem((1, 2, ROWS), F32),
            vmem((RING * PLACES, 2, ROWS), F32),
            pltpu.SemaphoreType.DMA((len(operands),)),
            pltpu.SemaphoreType.DMA((6,)),
            pltpu.SemaphoreType.DMA((6,)),
            pltpu.SemaphoreType.REGULAR((2,)),
        ],
        compiler_params=pltpu.CompilerParams(
            collective_id=0, has_side_effects=True, vmem_limit_bytes=40 * 1024 * 1024
        ),
        name="hyena_backward",
    )(*(pltpu.with_memory_space_constraint(x, pltpu.HBM) for x in operands))
    return pl.pallas_call(
        hand_over,
        out_shape=[jax.ShapeDtypeStruct(x.shape, x.dtype) for x in results],
        in_specs=[pl.BlockSpec(memory_space=pltpu.VMEM)] * 3,
        out_specs=[pl.BlockSpec(memory_space=pl.ANY)] * 3,
        scratch_shapes=[pltpu.SemaphoreType.DMA((3,))],
        name="hand_over",
    )(*(pltpu.with_memory_space_constraint(x, pltpu.VMEM) for x in results))


def solution(mesh):
    return jax.shard_map(
        local,
        mesh=mesh,
        in_specs=(P("seq", "ch"), P("seq", "ch"), P(), P(None, "ch"), P("ch"), P("ch")),
        out_specs=(P("seq", "ch"), P(None, "ch"), P()),
        check_vma=False,
    )
```

```python
import functools
import math

import jax
import jax.numpy as jnp
import ml_dtypes
import numpy as np
from jax import lax
from jax.experimental import pallas as pl
from jax.experimental.pallas import tpu as pltpu
from jax.sharding import PartitionSpec as P

F32 = jnp.float32
BF16 = jnp.bfloat16
BLOCKS = 32
ROWS = 128
OWN = 8
RUN = 4
CORES = 2
PLACES = 8
RING = 8
HID = 64
EMB = 32
LENGTH = BLOCKS * ROWS
PADDED = 2 * LENGTH
ROOT_HALF = math.sqrt(0.5)
OUTER = (
    [8 * m for m in range(5)]
    + [4 + 8 * m for m in range(4)]
    + [f + 8 * m for f in (1, 2, 3) for m in range(8)]
)
KEPT = len(OUTER)
PLACE = {k: n for n, k in enumerate(OUTER)}


def dot(a, b, contract=((1,), (0,))):
    return lax.dot_general(a, b, (contract, ((), ())), preferred_element_type=F32)


def halves(x):
    high = x.astype(BF16)
    return high, (x - high.astype(F32)).astype(BF16)


def fold(x):
    while x.shape[0] > 1:
        half = x.shape[0] // 2
        x = x[:half] + x[half:]
    return x


def np_halves(x):
    high = x.astype(ml_dtypes.bfloat16)
    low = (x - high.astype(np.float64)).astype(ml_dtypes.bfloat16)
    return high, low


@functools.cache
def tables():
    t = np.arange(LENGTH, dtype=np.int64)
    e = np.arange(EMB // 2, dtype=np.int64) + 1
    angle = (e[:, None] * t[None, :] % LENGTH).astype(np.float64) * (2 * math.pi / LENGTH)
    high, low = np_halves(np.concatenate([np.sin(angle), np.cos(angle)], axis=0))
    feats = np.concatenate([high, low, high], axis=0)
    columns = np.ascontiguousarray(np.concatenate([high, low], axis=0).T)
    n = np.arange(ROWS, dtype=np.int64)
    angle = (n[:, None] * n[None, :] % ROWS).astype(np.float64) * (2 * math.pi / ROWS)
    cos, sin = np.cos(angle), np.sin(angle)
    forward = np.block([[cos, -sin], [sin, cos]])
    back = np.block([[cos, sin], [-sin, cos]]) * (2.0 / PADDED)
    inner = np.stack([*np_halves(forward), *np_halves(back)])
    outer = np.array(OUTER, dtype=np.int64)
    angle = (outer[:, None] * n[None, :]).astype(np.float64) * (2 * math.pi / PADDED)
    turn = np.stack([np.cos(angle), np.sin(angle)]).astype(np.float32)
    turn = np.ascontiguousarray(np.broadcast_to(turn[:, :, None, :], (2, KEPT, OWN, ROWS)))
    return feats, columns, inner, turn


HALF_TURN = (3.140625, 9.67025756835937500e-4, 6.2771141529083251953e-7, 1.2154201256553420e-10)
SIN_SERIES = (1.0, -1 / 6, 1 / 120, -1 / 5040, 1 / 362880, -1 / 39916800)
COS_SERIES = (1.0, -1 / 2, 1 / 24, -1 / 720, 1 / 40320, -1 / 3628800, 1 / 479001600)


def series(coefs, x):
    total = jnp.full_like(x, coefs[-1])
    for coef in coefs[-2::-1]:
        total = total * x + coef
    return total


def sine_cosine(x):
    turns = jnp.round(x * (1 / math.pi))
    rest = x
    for part in HALF_TURN[:3]:
        rest = rest - turns * part
    half = turns * 0.5
    sign = 1.0 - 4.0 * jnp.abs(half - jnp.round(half))
    square = rest * rest
    return sign * rest * series(SIN_SERIES, square), sign * series(COS_SERIES, square)


def c_add(a, b):
    return tuple(p if q is None else q if p is None else p + q for p, q in zip(a, b))


def c_neg(a):
    return tuple(None if p is None else -p for p in a)


def c_sub(a, b):
    return tuple(
        p if q is None else -q if p is None else p - q for p, q in zip(a, b)
    )


def c_turn(a, number, count):
    number = number % count
    if number == 0:
        return a
    if 2 * number == count:
        return c_neg(a)
    re, im = a
    if 4 * number == count:
        return (None if im is None else -im, re)
    if 4 * number == 3 * count:
        return (im, None if re is None else -re)
    cos, sin = math.cos(2 * math.pi * number / count), math.sin(2 * math.pi * number / count)
    if im is None:
        return (re * cos, re * sin)
    if 8 * number == count:
        return ((re - im) * ROOT_HALF, (re + im) * ROOT_HALF)
    if 8 * number == 7 * count:
        return ((re + im) * ROOT_HALF, (im - re) * ROOT_HALF)
    if 8 * number == 3 * count:
        return ((re + im) * -ROOT_HALF, (re - im) * ROOT_HALF)
    if 8 * number == 5 * count:
        return ((im - re) * ROOT_HALF, (re + im) * -ROOT_HALF)
    return (re * cos - im * sin, re * sin + im * cos)


def transform(values, sign):
    count = len(values)
    if count == 1:
        return list(values)
    even, odd = transform(values[::2], sign), transform(values[1::2], sign)
    odd = [c_turn(v, sign * k, count) for k, v in enumerate(odd)]
    return [c_add(a, b) for a, b in zip(even, odd)] + [c_sub(a, b) for a, b in zip(even, odd)]


def outer_forward(x):
    parts = [[None] * 8 for _ in range(5)]
    for b in range(8):
        x0, x1, x2, x3 = x[b], x[8 + b], x[16 + b], x[24 + b]
        plus, minus, other, differ = x0 + x2, x0 - x2, x1 + x3, x1 - x3
        part, whole = differ * ROOT_HALF, other * ROOT_HALF
        parts[0][b] = (plus + other, None)
        parts[4][b] = (plus - other, None)
        parts[2][b] = (minus, -differ)
        parts[1][b] = (x0 + part, -(x2 + whole))
        parts[3][b] = (x0 - part, x2 - whole)
    for f, count in ((0, 5), (4, 4), (1, 8), (2, 8), (3, 8)):
        turned = [c_turn(v, -b * f, 64) for b, v in enumerate(parts[f])]
        yield from transform(turned, -1)[:count]


def outer_back(z):
    z = {k: z[n] for n, k in enumerate(OUTER)}
    s = ROOT_HALF
    ends, sides = z[0][0] + z[32][0], z[0][0] - z[32][0]
    (r1, i1), (r2, i2), (r3, i3) = z[8], z[16], z[24]
    one, two = s * ((r1 - i1) - (r3 + i3)), s * ((r3 - i3) - (r1 + i1))
    rsum, idiff = r1 + r3, i3 - i1
    v0 = [
        ends + r2 + rsum,
        sides - i2 + one,
        ends - r2 + idiff,
        sides + i2 + two,
        ends + r2 - rsum,
        sides - i2 - one,
        ends - r2 - idiff,
        sides + i2 - two,
    ]
    quarter = [z[4 + 8 * m] for m in range(4)]
    even = transform(quarter, 1)
    odd = transform([c_turn(v, m, 8) for m, v in enumerate(quarter)], 1)
    v4 = []
    for b in range(8):
        re, im = (odd if b % 2 else even)[b // 2]
        angle = 2 * math.pi * b / 16
        v4.append(re if b == 0 else re * math.cos(angle) - im * math.sin(angle))
    v1, v2, v3 = (
        [c_turn(v, b * f, 64) for b, v in enumerate(transform([z[f + 8 * m] for m in range(8)], 1))]
        for f in (1, 2, 3)
    )
    y = [None] * BLOCKS
    for b in range(8):
        (r1, i1), (r2, i2), (r3, i3) = v1[b], v2[b], v3[b]
        ends, sides = v0[b] + v4[b], v0[b] - v4[b]
        y[b] = ends + r2 + (r1 + r3)
        y[8 + b] = sides - i2 + s * ((r1 - i1) - (r3 + i3))
        y[16 + b] = ends - r2 + (i3 - i1)
        y[24 + b] = sides + i2 + s * ((r3 - i3) - (r1 + i1))
    return y


def spectrum(load, turn, inner, spec):
    done = 0
    for n, (re, im) in enumerate(outer_forward([load(b) for b in range(BLOCKS)])):
        cos, sin = turn[0, n], turn[1, n]
        spec[n, :, :ROWS] = re * cos if im is None else re * cos + im * sin
        spec[n, :, ROWS:] = -(re * sin) if im is None else im * cos - re * sin
        if n + 1 in (KEPT // 2 + 1, KEPT):
            inner_forward(spec.at[pl.ds(done, n + 1 - done)], inner)
            done = n + 1


def gather(spec, turn):
    z = []
    for n, k in enumerate(OUTER):
        re, im, cos, sin = spec[n, :, :ROWS], spec[n, :, ROWS:], turn[0, n], turn[1, n]
        re, im = re * cos - im * sin, im * cos + re * sin
        z.append((re * 0.5, im * 0.5) if k in (0, 32) else (re, im))
    return outer_back(z)


def inner_pass(x, high, low):
    x_high, x_low = halves(x)
    return dot(x_high, high) + dot(x_low, high) + dot(x_high, low)


def inner_forward(spec, inner):
    x = spec[...].reshape(-1, 2 * ROWS)
    spec[...] = inner_pass(x, inner[0], inner[1]).reshape(-1, OWN, 2 * ROWS)


def inner_back(left, right, spec, inner):
    lr, li = left[:, :, :ROWS], left[:, :, ROWS:]
    rr, ri = right[:, :, :ROWS], right[:, :, ROWS:]
    re = (lr * rr + li * ri).reshape(KEPT * OWN, ROWS)
    im = (li * rr - lr * ri).reshape(KEPT * OWN, ROWS)
    x = jnp.concatenate([re, im], axis=1)
    spec[...] = inner_pass(x, inner[2], inner[3]).reshape(KEPT, OWN, 2 * ROWS)


def kernel(
    u_in, g_in, ew_in, fw_in, rate_in, gain_in, feats_in, columns_in, inner_in, turn_in,
    sig_out, fgrad_out, egrad_out,
    u, g, ew, fw, rate_row, gain_row, feats, columns, inner, turn,
    send_u, recv_u, send_g, recv_g, own_par, pre, active, slopes, base, filt, decays,
    spec_f, spec_u, spec_g, spec_y, bg, weights,
    send_s, recv_s, send_f, recv_f, part1, recv1, part2, recv2,
    in_sem, send_sem, recv_sem, ready,
):
    me, group = lax.axis_index("seq"), lax.axis_index("ch")
    core, y_low, x = lax.rem(me, CORES), lax.rem(lax.div(me, CORES), RUN), lax.div(me, CORES * RUN)
    z, y_high = lax.rem(group, RING), lax.div(group, RING)
    y, place = y_high * RUN + y_low, x * CORES + core

    steps = (4, 5, 3, 6, 2, 7, 1, 0)
    there = {n: lax.rem(place + n, PLACES) for n in steps}
    first = {n: lax.div(p, CORES) * (CORES * RUN) + lax.rem(p, CORES) for n, p in there.items()}

    def other_blocks(*bodies):
        rows = [lax.select(y_low == 0, RUN - 1 - n, n + (n >= y_low).astype(jnp.int32)) for n in range(RUN - 1)]
        rows.append(y_low)
        for number, row in enumerate(rows):
            seqs = [first[n] + CORES * row for n in steps if n or number < RUN - 1]
            for one in bodies:
                for seq in seqs:
                    one(seq, {"seq": seq})

    def others_along(own, order, device_of, body):
        for index in order:
            for n in steps[:-1]:
                body(there[n], device_of(n, index))

            @pl.when(own != index)
            def _():
                body(place, device_of(0, index))

    def other_y(body):
        def device(n, index):
            return {"seq": first[n] + CORES * (index % RUN), "ch": index // RUN * RING + z}

        others_along(y, (0, 1, 7, 2, 6, 3, 5, 4), device, body)

    def other_z(body):
        def device(n, index):
            return {"seq": first[n] + CORES * y_low, "ch": y_high * RING + index}

        others_along(z, range(RING), device, body)

    barrier = pltpu.get_barrier_semaphore()

    def along_z(n):
        return {"ch": y_high * RING + lax.rem(z + n, RING)}

    second = [along_z(2), along_z(RING - 2)]
    relays = [{"ch": (1 - y_high) * RING + z}, *second, along_z(1), along_z(RING - 1)]

    other_blocks(lambda _, device: pl.semaphore_signal(barrier, inc=1, device_id=device))
    for device in relays:
        pl.semaphore_signal(barrier, inc=1, device_id=device)

    pairs = (
        (u_in, u), (g_in, g), (ew_in, ew), (fw_in, fw), (rate_in, rate_row), (gain_in, gain_row),
        (feats_in, feats), (columns_in, columns), (inner_in, inner), (turn_in, turn),
    )
    loads = [pltpu.make_async_copy(a, b, in_sem.at[n]) for n, (a, b) in enumerate(pairs)]
    for load in loads:
        load.start()

    def send(n, others, own, source, target):
        others(sender(n, own, source, target))

    def sender(n, own, source, target):
        def one(there, device):
            pltpu.make_async_remote_copy(
                src_ref=source(there),
                dst_ref=target.at[own],
                send_sem=send_sem.at[n],
                recv_sem=recv_sem.at[n],
                device_id=device,
            ).start()

        return one

    def wait(sem, n, ref, count):
        part = ref.at[pl.ds(0, count)]
        pltpu.make_async_copy(part, part, sem.at[n]).wait()

    loads[0].wait()
    loads[1].wait()
    for x_ref, send_ref in ((u, send_u), (g, send_g)):
        send_ref[...] = x_ref[...].astype(F32).T.reshape(BLOCKS, OWN, ROWS).astype(BF16)
    pl.semaphore_wait(barrier, BLOCKS - 1 + len(relays))
    other_blocks(
        sender(0, me, lambda there: send_u.at[there], recv_u),
        sender(5, me, lambda there: send_g.at[there], recv_g),
    )
    recv_u[pl.ds(me, 1)] = send_u[pl.ds(me, 1)]
    recv_g[pl.ds(me, 1)] = send_g[pl.ds(me, 1)]
    for device in relays:
        pl.semaphore_signal(ready.at[0], inc=1, device_id=device)

    for load in loads[2:]:
        load.wait()
    own_par[:, :HID] = fw[...].T
    own_par[:, HID : HID + 8] = jnp.broadcast_to(rate_row[...], (8, BLOCKS * OWN)).T
    own_par[:, HID + 8 : HID + 16] = jnp.broadcast_to(gain_row[...], (8, BLOCKS * OWN)).T
    par = own_par[pl.ds(pl.multiple_of(me * OWN, OWN), OWN), :]
    weight = par[:, :HID]
    rate = jnp.broadcast_to(par[:, HID : HID + 1], (OWN, ROWS))
    gain = jnp.broadcast_to(par[:, HID + 8 : HID + 9], (OWN, ROWS))
    w_high, w_low = halves(weight)

    e_high, e_low = halves(ew[...].T)
    pre[...] = dot(jnp.concatenate([e_high, e_high, e_low], axis=1), feats[...])

    @pl.loop(0, LENGTH // 256)
    def _(n):
        part = pl.ds(pl.multiple_of(n * 256, 256), 256)
        sine, cosine = sine_cosine(pre[:, part])
        high, low = halves(sine)
        active[:HID, part] = high
        active[HID:, part] = low
        slopes[:, part] = cosine

    stacked = jnp.concatenate(
        [
            jnp.concatenate([w_high.astype(F32), w_high.astype(F32)], axis=1),
            jnp.concatenate([w_low.astype(F32), jnp.zeros((OWN, HID), F32)], axis=1),
        ],
        axis=0,
    ).astype(BF16)
    base[...] = dot(stacked, active[...])

    w_left, w_right = w_high.astype(F32), w_low.astype(F32)
    tall = jnp.concatenate([w_left, w_left, w_right, jnp.zeros_like(w_left)], axis=0)
    weights[...] = tall.T.astype(BF16)

    lanes = lax.broadcasted_iota(jnp.int32, (OWN, ROWS), 1)
    for b in range(BLOCKS):
        part = slice(b * ROWS, (b + 1) * ROWS)
        decay = jnp.exp(-rate * (lanes + b * ROWS).astype(F32) / LENGTH)
        decays[b] = decay
        value = (base[:OWN, part] + base[OWN:, part]) * decay
        filt[b] = value.astype(BF16).astype(F32)
    spectrum(lambda b: filt[b], turn, inner, spec_f)

    wait(recv_sem, 0, recv_u, BLOCKS - 1)
    spectrum(lambda b: recv_u[b].astype(F32), turn, inner, spec_u)
    wait(recv_sem, 5, recv_g, BLOCKS - 1)
    spectrum(lambda b: recv_g[b].astype(F32), turn, inner, spec_g)

    inner_back(spec_g, spec_u, spec_y, inner)
    for b, lag in enumerate(gather(spec_y, turn)):
        grad = lag * decays[b]
        high = grad.astype(BF16).astype(F32)
        pair = jnp.concatenate([high, grad - high], axis=0).astype(BF16)
        bg[: 2 * OWN, b * ROWS : (b + 1) * ROWS] = pair
        bg[2 * OWN :, b * ROWS : (b + 1) * ROWS] = pair
    q_high, q_low = halves(dot(weights[...], bg[...]) * slopes[...])
    parts = dot(jnp.concatenate([q_high, q_low], axis=0), columns[...])
    embed = (parts[:HID, :EMB] + parts[:HID, EMB:] + parts[HID:, :EMB]).T
    packed = jnp.concatenate([embed[: EMB // 2], embed[EMB // 2 :]], axis=1)
    for n in range(PLACES):
        part1[n] = packed[2 * n : 2 * n + 2]
    pl.semaphore_wait(ready.at[0], len(relays))
    slot = y * PLACES + place
    send(1, other_y, slot, lambda there: part1.at[there], recv1)
    recv1[pl.ds(slot, 1)] = part1[pl.ds(place, 1)]
    for device in second:
        pl.semaphore_signal(ready.at[1], inc=1, device_id=device)

    inner_back(spec_g, spec_f, spec_y, inner)
    for b, conv in enumerate(gather(spec_y, turn)):
        send_s[b] = (conv + gain * recv_g[b].astype(F32)).astype(BF16)
    send(2, other_blocks, me, lambda there: send_s.at[there], recv_s)
    recv_s[pl.ds(me, 1)] = send_s[pl.ds(me, 1)]

    parts = dot(bg[: 2 * OWN], active[...], ((1,), (1,)))
    fgrad = (parts[:OWN, :HID] + parts[:OWN, HID:] + parts[OWN:, :HID]) * (1.0 / LENGTH)
    send_f[0] = jnp.concatenate([fgrad[: OWN // 2], fgrad[OWN // 2 :]], axis=1)
    send(4, other_blocks, me, lambda there: send_f.at[0], recv_f)
    recv_f[pl.ds(me, 1)] = send_f[...]

    wait(recv_sem, 1, recv1, RING * PLACES - 1)
    part2[...] = fold(recv1[...]) * (1.0 / math.sqrt(LENGTH))
    slot = place * RING + z
    pl.semaphore_wait(ready.at[1], len(second))
    send(3, other_z, slot, lambda there: part2.at[0], recv2)
    recv2[pl.ds(slot, 1)] = part2[...]

    wait(recv_sem, 2, recv_s, BLOCKS - 1)
    sig_out[...] = recv_s[...].astype(F32).reshape(BLOCKS * OWN, ROWS).T.astype(BF16)

    wait(recv_sem, 4, recv_f, BLOCKS - 1)
    pieces = recv_f[...]
    fgrad_out[...] = (
        jnp.concatenate([pieces[:, :, :HID], pieces[:, :, HID:]], axis=1).reshape(BLOCKS * OWN, HID).T
    )

    wait(send_sem, 0, send_u, BLOCKS - 1)
    wait(send_sem, 5, send_g, BLOCKS - 1)
    wait(send_sem, 1, recv1, RING * PLACES - 1)
    wait(send_sem, 2, send_s, BLOCKS - 1)
    wait(send_sem, 3, recv2, RING * PLACES - 1)
    wait(send_sem, 4, recv_f, BLOCKS - 1)

    wait(recv_sem, 3, recv2, RING * PLACES - 1)
    for n in range(PLACES):
        piece = fold(recv2[n * RING : (n + 1) * RING])[0]
        egrad_out[2 * n : 2 * n + 2] = piece[:, :HID]
        egrad_out[EMB // 2 + 2 * n : EMB // 2 + 2 * n + 2] = piece[:, HID:]


def hand_over(*refs):
    copies = [pltpu.make_async_copy(refs[n], refs[3 + n], refs[6].at[n]) for n in range(3)]
    for copy in copies:
        copy.start()
    for copy in copies:
        copy.wait()


def local(inputs, out_grad, embed_weight, filter_weight, decay_rate, skip_gain):
    channels = inputs.shape[1]
    feats, columns, inner, turn = tables()
    operands = (
        inputs,
        out_grad,
        embed_weight,
        filter_weight,
        decay_rate.reshape(1, channels),
        skip_gain.reshape(1, channels),
        jnp.asarray(feats),
        jnp.asarray(columns),
        jnp.asarray(inner),
        jnp.asarray(turn),
    )
    vmem = pltpu.VMEM
    results = pl.pallas_call(
        kernel,
        out_shape=(
            pltpu.VMEM((ROWS, channels), BF16),
            pltpu.VMEM((HID, channels), F32),
            pltpu.VMEM((EMB, HID), F32),
        ),
        in_specs=[pl.BlockSpec(memory_space=pltpu.HBM)] * len(operands),
        out_specs=[pl.BlockSpec(memory_space=pltpu.VMEM)] * 3,
        scratch_shapes=[vmem(x.shape, x.dtype) for x in operands]
        + [
            vmem((BLOCKS, OWN, ROWS), BF16),
            vmem((BLOCKS, OWN, ROWS), BF16),
            vmem((BLOCKS, OWN, ROWS), BF16),
            vmem((BLOCKS, OWN, ROWS), BF16),
            vmem((channels, ROWS), F32),
            vmem((HID, LENGTH), F32),
            vmem((2 * HID, LENGTH), BF16),
            vmem((HID, LENGTH), F32),
            vmem((2 * OWN, LENGTH), F32),
            vmem((BLOCKS, OWN, ROWS), F32),
            vmem((BLOCKS, OWN, ROWS), F32),
            vmem((KEPT, OWN, 2 * ROWS), F32),
            vmem((KEPT, OWN, 2 * ROWS), F32),
            vmem((KEPT, OWN, 2 * ROWS), F32),
            vmem((KEPT, OWN, 2 * ROWS), F32),
            vmem((4 * OWN, LENGTH), BF16),
            vmem((HID, 4 * OWN), BF16),
            vmem((BLOCKS, OWN, ROWS), BF16),
            vmem((BLOCKS, OWN, ROWS), BF16),
            vmem((1, OWN // 2, ROWS), F32),
            vmem((BLOCKS, OWN // 2, ROWS), F32),
            vmem((PLACES, 2, ROWS), F32),
            vmem((RING * PLACES, 2, ROWS), F32),
            vmem((1, 2, ROWS), F32),
            vmem((RING * PLACES, 2, ROWS), F32),
            pltpu.SemaphoreType.DMA((len(operands),)),
            pltpu.SemaphoreType.DMA((6,)),
            pltpu.SemaphoreType.DMA((6,)),
            pltpu.SemaphoreType.REGULAR((2,)),
        ],
        compiler_params=pltpu.CompilerParams(
            collective_id=0, has_side_effects=True, vmem_limit_bytes=40 * 1024 * 1024
        ),
        name="hyena_backward",
    )(*(pltpu.with_memory_space_constraint(x, pltpu.HBM) for x in operands))
    return pl.pallas_call(
        hand_over,
        out_shape=[jax.ShapeDtypeStruct(x.shape, x.dtype) for x in results],
        in_specs=[pl.BlockSpec(memory_space=pltpu.VMEM)] * 3,
        out_specs=[pl.BlockSpec(memory_space=pl.ANY)] * 3,
        scratch_shapes=[pltpu.SemaphoreType.DMA((3,))],
        name="hand_over",
    )(*(pltpu.with_memory_space_constraint(x, pltpu.VMEM) for x in results))


def solution(mesh):
    return jax.shard_map(
        local,
        mesh=mesh,
        in_specs=(P("seq", "ch"), P("seq", "ch"), P(), P(None, "ch"), P("ch"), P("ch")),
        out_specs=(P("seq", "ch"), P(None, "ch"), P()),
        check_vma=False,
    )
```

```python
import functools
import math

import jax
import jax.numpy as jnp
import ml_dtypes
import numpy as np
from jax import lax
from jax.experimental import pallas as pl
from jax.experimental.pallas import tpu as pltpu
from jax.sharding import PartitionSpec as P

F32 = jnp.float32
BF16 = jnp.bfloat16
BLOCKS = 32
ROWS = 128
OWN = 8
RUN = 4
CORES = 2
PLACES = 8
RING = 8
HID = 64
EMB = 32
LENGTH = BLOCKS * ROWS
PADDED = 2 * LENGTH
ROOT_HALF = math.sqrt(0.5)
OUTER = (
    [8 * m for m in range(5)]
    + [4 + 8 * m for m in range(4)]
    + [f + 8 * m for f in (1, 2, 3) for m in range(8)]
)
KEPT = len(OUTER)
PLACE = {k: n for n, k in enumerate(OUTER)}


def dot(a, b, contract=((1,), (0,))):
    return lax.dot_general(a, b, (contract, ((), ())), preferred_element_type=F32)


def halves(x):
    high = x.astype(BF16)
    return high, (x - high.astype(F32)).astype(BF16)


def fold(x):
    while x.shape[0] > 1:
        half = x.shape[0] // 2
        x = x[:half] + x[half:]
    return x


def np_halves(x):
    high = x.astype(ml_dtypes.bfloat16)
    low = (x - high.astype(np.float64)).astype(ml_dtypes.bfloat16)
    return high, low


@functools.cache
def tables():
    t = np.arange(LENGTH, dtype=np.int64)
    e = np.arange(EMB // 2, dtype=np.int64) + 1
    angle = (e[:, None] * t[None, :] % LENGTH).astype(np.float64) * (2 * math.pi / LENGTH)
    high, low = np_halves(np.concatenate([np.sin(angle), np.cos(angle)], axis=0))
    feats = np.concatenate([high, low, high], axis=0)
    columns = np.ascontiguousarray(np.concatenate([high, low], axis=0).T)
    n = np.arange(ROWS, dtype=np.int64)
    angle = (n[:, None] * n[None, :] % ROWS).astype(np.float64) * (2 * math.pi / ROWS)
    cos, sin = np.cos(angle), np.sin(angle)
    forward = np.block([[cos, -sin], [sin, cos]])
    back = np.block([[cos, sin], [-sin, cos]]) * (2.0 / PADDED)
    inner = np.stack([*np_halves(forward), *np_halves(back)])
    outer = np.array(OUTER, dtype=np.int64)
    angle = (outer[:, None] * n[None, :]).astype(np.float64) * (2 * math.pi / PADDED)
    turn = np.stack([np.cos(angle), np.sin(angle)]).astype(np.float32)
    turn = np.ascontiguousarray(np.broadcast_to(turn[:, :, None, :], (2, KEPT, OWN, ROWS)))
    return feats, columns, inner, turn


HALF_TURN = (3.140625, 9.67025756835937500e-4, 6.2771141529083251953e-7, 1.2154201256553420e-10)
SIN_SERIES = (1.0, -1 / 6, 1 / 120, -1 / 5040, 1 / 362880, -1 / 39916800)
COS_SERIES = (1.0, -1 / 2, 1 / 24, -1 / 720, 1 / 40320, -1 / 3628800, 1 / 479001600)


def series(coefs, x):
    total = jnp.full_like(x, coefs[-1])
    for coef in coefs[-2::-1]:
        total = total * x + coef
    return total


def sine_cosine(x):
    turns = jnp.round(x * (1 / math.pi))
    rest = x
    for part in HALF_TURN[:3]:
        rest = rest - turns * part
    half = turns * 0.5
    sign = 1.0 - 4.0 * jnp.abs(half - jnp.round(half))
    square = rest * rest
    return sign * rest * series(SIN_SERIES, square), sign * series(COS_SERIES, square)


def c_add(a, b):
    return tuple(p if q is None else q if p is None else p + q for p, q in zip(a, b))


def c_neg(a):
    return tuple(None if p is None else -p for p in a)


def c_sub(a, b):
    return tuple(
        p if q is None else -q if p is None else p - q for p, q in zip(a, b)
    )


def c_turn(a, number, count):
    number = number % count
    if number == 0:
        return a
    if 2 * number == count:
        return c_neg(a)
    re, im = a
    if 4 * number == count:
        return (None if im is None else -im, re)
    if 4 * number == 3 * count:
        return (im, None if re is None else -re)
    cos, sin = math.cos(2 * math.pi * number / count), math.sin(2 * math.pi * number / count)
    if im is None:
        return (re * cos, re * sin)
    if 8 * number == count:
        return ((re - im) * ROOT_HALF, (re + im) * ROOT_HALF)
    if 8 * number == 7 * count:
        return ((re + im) * ROOT_HALF, (im - re) * ROOT_HALF)
    if 8 * number == 3 * count:
        return ((re + im) * -ROOT_HALF, (re - im) * ROOT_HALF)
    if 8 * number == 5 * count:
        return ((im - re) * ROOT_HALF, (re + im) * -ROOT_HALF)
    return (re * cos - im * sin, re * sin + im * cos)


def transform(values, sign):
    count = len(values)
    if count == 1:
        return list(values)
    even, odd = transform(values[::2], sign), transform(values[1::2], sign)
    odd = [c_turn(v, sign * k, count) for k, v in enumerate(odd)]
    return [c_add(a, b) for a, b in zip(even, odd)] + [c_sub(a, b) for a, b in zip(even, odd)]


def outer_forward(x):
    parts = [[None] * 8 for _ in range(5)]
    for b in range(8):
        x0, x1, x2, x3 = x[b], x[8 + b], x[16 + b], x[24 + b]
        plus, minus, other, differ = x0 + x2, x0 - x2, x1 + x3, x1 - x3
        part, whole = differ * ROOT_HALF, other * ROOT_HALF
        parts[0][b] = (plus + other, None)
        parts[4][b] = (plus - other, None)
        parts[2][b] = (minus, -differ)
        parts[1][b] = (x0 + part, -(x2 + whole))
        parts[3][b] = (x0 - part, x2 - whole)
    found = {}
    for f in range(5):
        turned = [c_turn(v, -b * f, 64) for b, v in enumerate(parts[f])]
        for m, v in enumerate(transform(turned, -1)):
            found[f + 8 * m] = v
    return [found[k] for k in OUTER]


def outer_back(z):
    z = {k: z[n] for n, k in enumerate(OUTER)}
    s = ROOT_HALF
    ends, sides = z[0][0] + z[32][0], z[0][0] - z[32][0]
    (r1, i1), (r2, i2), (r3, i3) = z[8], z[16], z[24]
    one, two = s * ((r1 - i1) - (r3 + i3)), s * ((r3 - i3) - (r1 + i1))
    rsum, idiff = r1 + r3, i3 - i1
    v0 = [
        ends + r2 + rsum,
        sides - i2 + one,
        ends - r2 + idiff,
        sides + i2 + two,
        ends + r2 - rsum,
        sides - i2 - one,
        ends - r2 - idiff,
        sides + i2 - two,
    ]
    quarter = [z[4 + 8 * m] for m in range(4)]
    even = transform(quarter, 1)
    odd = transform([c_turn(v, m, 8) for m, v in enumerate(quarter)], 1)
    v4 = []
    for b in range(8):
        re, im = (odd if b % 2 else even)[b // 2]
        angle = 2 * math.pi * b / 16
        v4.append(re if b == 0 else re * math.cos(angle) - im * math.sin(angle))
    v1, v2, v3 = (
        [c_turn(v, b * f, 64) for b, v in enumerate(transform([z[f + 8 * m] for m in range(8)], 1))]
        for f in (1, 2, 3)
    )
    y = [None] * BLOCKS
    for b in range(8):
        (r1, i1), (r2, i2), (r3, i3) = v1[b], v2[b], v3[b]
        ends, sides = v0[b] + v4[b], v0[b] - v4[b]
        y[b] = ends + r2 + (r1 + r3)
        y[8 + b] = sides - i2 + s * ((r1 - i1) - (r3 + i3))
        y[16 + b] = ends - r2 + (i3 - i1)
        y[24 + b] = sides + i2 + s * ((r3 - i3) - (r1 + i1))
    return y


def spread(load, turn, spec):
    for n, (re, im) in enumerate(outer_forward([load(b) for b in range(BLOCKS)])):
        cos, sin = turn[0, n], turn[1, n]
        spec[n, :, :ROWS] = re * cos if im is None else re * cos + im * sin
        spec[n, :, ROWS:] = -(re * sin) if im is None else im * cos - re * sin


def gather(spec, turn):
    z = []
    for n, k in enumerate(OUTER):
        re, im, cos, sin = spec[n, :, :ROWS], spec[n, :, ROWS:], turn[0, n], turn[1, n]
        re, im = re * cos - im * sin, im * cos + re * sin
        z.append((re * 0.5, im * 0.5) if k in (0, 32) else (re, im))
    return outer_back(z)


def inner_pass(x, high, low):
    x_high, x_low = halves(x)
    return dot(x_high, high) + dot(x_low, high) + dot(x_high, low)


def inner_forward(spec, inner):
    x = spec[...].reshape(KEPT * OWN, 2 * ROWS)
    spec[...] = inner_pass(x, inner[0], inner[1]).reshape(KEPT, OWN, 2 * ROWS)


def inner_back(left, right, spec, inner):
    lr, li = left[:, :, :ROWS], left[:, :, ROWS:]
    rr, ri = right[:, :, :ROWS], right[:, :, ROWS:]
    re = (lr * rr + li * ri).reshape(KEPT * OWN, ROWS)
    im = (li * rr - lr * ri).reshape(KEPT * OWN, ROWS)
    x = jnp.concatenate([re, im], axis=1)
    spec[...] = inner_pass(x, inner[2], inner[3]).reshape(KEPT, OWN, 2 * ROWS)


def kernel(
    u_in, g_in, ew_in, fw_in, rate_in, gain_in, feats_in, columns_in, inner_in, turn_in,
    sig_out, fgrad_out, egrad_out,
    u, g, ew, fw, rate_row, gain_row, feats, columns, inner, turn,
    send_u, recv_u, send_g, recv_g, own_par, pre, active, slopes, base, filt, decays,
    spec_f, spec_u, spec_g, spec_y, bg, weights,
    send_s, recv_s, send_f, recv_f, part1, recv1, part2, recv2,
    in_sem, send_sem, recv_sem, ready,
):
    me, group = lax.axis_index("seq"), lax.axis_index("ch")
    core, y_low, x = lax.rem(me, CORES), lax.rem(lax.div(me, CORES), RUN), lax.div(me, CORES * RUN)
    z, y_high = lax.rem(group, RING), lax.div(group, RING)
    y, place = y_high * RUN + y_low, x * CORES + core

    steps = (4, 5, 3, 6, 2, 7, 1, 0)
    there = {n: lax.rem(place + n, PLACES) for n in steps}
    first = {n: lax.div(p, CORES) * (CORES * RUN) + lax.rem(p, CORES) for n, p in there.items()}

    def other_blocks(*bodies):
        rows = [lax.select(y_low == 0, RUN - 1 - n, n + (n >= y_low).astype(jnp.int32)) for n in range(RUN - 1)]
        rows.append(y_low)
        for number, row in enumerate(rows):
            seqs = [first[n] + CORES * row for n in steps if n or number < RUN - 1]
            for one in bodies:
                for seq in seqs:
                    one(seq, {"seq": seq})

    def others_along(own, order, device_of, body):
        for index in order:
            for n in steps[:-1]:
                body(there[n], device_of(n, index))

            @pl.when(own != index)
            def _():
                body(place, device_of(0, index))

    def other_y(body):
        def device(n, index):
            return {"seq": first[n] + CORES * (index % RUN), "ch": index // RUN * RING + z}

        others_along(y, (0, 7, 1, 6, 5, 4, 2, 3), device, body)

    def other_z(body):
        def device(n, index):
            return {"seq": first[n] + CORES * y_low, "ch": y_high * RING + index}

        others_along(z, (0, 7, 1, 6, 5, 4, 2, 3), device, body)

    barrier = pltpu.get_barrier_semaphore()

    def along_z(n):
        return {"ch": y_high * RING + lax.rem(z + n, RING)}

    second = [along_z(2), along_z(RING - 2)]
    relays = [{"ch": (1 - y_high) * RING + z}, *second, along_z(1), along_z(RING - 1)]

    other_blocks(lambda _, device: pl.semaphore_signal(barrier, inc=1, device_id=device))
    for device in relays:
        pl.semaphore_signal(barrier, inc=1, device_id=device)

    pairs = (
        (u_in, u), (g_in, g), (ew_in, ew), (fw_in, fw), (rate_in, rate_row), (gain_in, gain_row),
        (feats_in, feats), (columns_in, columns), (inner_in, inner), (turn_in, turn),
    )
    loads = [pltpu.make_async_copy(a, b, in_sem.at[n]) for n, (a, b) in enumerate(pairs)]
    for load in loads:
        load.start()

    def send(n, others, own, source, target):
        others(sender(n, own, source, target))

    def sender(n, own, source, target):
        def one(there, device):
            pltpu.make_async_remote_copy(
                src_ref=source(there),
                dst_ref=target.at[own],
                send_sem=send_sem.at[n],
                recv_sem=recv_sem.at[n],
                device_id=device,
            ).start()

        return one

    def wait(sem, n, ref, count):
        part = ref.at[pl.ds(0, count)]
        pltpu.make_async_copy(part, part, sem.at[n]).wait()

    loads[0].wait()
    loads[1].wait()
    for x_ref, send_ref in ((u, send_u), (g, send_g)):
        send_ref[...] = x_ref[...].astype(F32).T.reshape(BLOCKS, OWN, ROWS).astype(BF16)
    pl.semaphore_wait(barrier, BLOCKS - 1 + len(relays))
    other_blocks(
        sender(0, me, lambda there: send_u.at[there], recv_u),
        sender(5, me, lambda there: send_g.at[there], recv_g),
    )
    recv_u[pl.ds(me, 1)] = send_u[pl.ds(me, 1)]
    recv_g[pl.ds(me, 1)] = send_g[pl.ds(me, 1)]
    for device in relays:
        pl.semaphore_signal(ready.at[0], inc=1, device_id=device)

    for load in loads[2:]:
        load.wait()
    own_par[:, :HID] = fw[...].T
    own_par[:, HID : HID + 8] = jnp.broadcast_to(rate_row[...], (8, BLOCKS * OWN)).T
    own_par[:, HID + 8 : HID + 16] = jnp.broadcast_to(gain_row[...], (8, BLOCKS * OWN)).T
    par = own_par[pl.ds(pl.multiple_of(me * OWN, OWN), OWN), :]
    weight = par[:, :HID]
    rate = jnp.broadcast_to(par[:, HID : HID + 1], (OWN, ROWS))
    gain = jnp.broadcast_to(par[:, HID + 8 : HID + 9], (OWN, ROWS))
    w_high, w_low = halves(weight)

    e_high, e_low = halves(ew[...].T)
    pre[...] = dot(jnp.concatenate([e_high, e_high, e_low], axis=1), feats[...])

    @pl.loop(0, LENGTH // 256)
    def _(n):
        part = pl.ds(pl.multiple_of(n * 256, 256), 256)
        sine, cosine = sine_cosine(pre[:, part])
        high, low = halves(sine)
        active[:HID, part] = high
        active[HID:, part] = low
        slopes[:, part] = cosine

    stacked = jnp.concatenate(
        [
            jnp.concatenate([w_high.astype(F32), w_high.astype(F32)], axis=1),
            jnp.concatenate([w_low.astype(F32), jnp.zeros((OWN, HID), F32)], axis=1),
        ],
        axis=0,
    ).astype(BF16)
    base[...] = dot(stacked, active[...])

    w_left, w_right = w_high.astype(F32), w_low.astype(F32)
    tall = jnp.concatenate([w_left, w_left, w_right, jnp.zeros_like(w_left)], axis=0)
    weights[...] = tall.T.astype(BF16)

    lanes = lax.broadcasted_iota(jnp.int32, (OWN, ROWS), 1)
    for b in range(BLOCKS):
        part = slice(b * ROWS, (b + 1) * ROWS)
        decay = jnp.exp(-rate * (lanes + b * ROWS).astype(F32) / LENGTH)
        decays[b] = decay
        value = (base[:OWN, part] + base[OWN:, part]) * decay
        filt[b] = value.astype(BF16).astype(F32)
    spread(lambda b: filt[b], turn, spec_f)
    inner_forward(spec_f, inner)

    wait(recv_sem, 0, recv_u, BLOCKS - 1)
    spread(lambda b: recv_u[b].astype(F32), turn, spec_u)
    inner_forward(spec_u, inner)
    wait(recv_sem, 5, recv_g, BLOCKS - 1)
    spread(lambda b: recv_g[b].astype(F32), turn, spec_g)
    inner_forward(spec_g, inner)

    inner_back(spec_g, spec_u, spec_y, inner)
    for b, lag in enumerate(gather(spec_y, turn)):
        grad = lag * decays[b]
        high = grad.astype(BF16).astype(F32)
        pair = jnp.concatenate([high, grad - high], axis=0).astype(BF16)
        bg[: 2 * OWN, b * ROWS : (b + 1) * ROWS] = pair
        bg[2 * OWN :, b * ROWS : (b + 1) * ROWS] = pair
    q_high, q_low = halves(dot(weights[...], bg[...]) * slopes[...])
    parts, low = dot(q_high, columns[...]), dot(q_low, columns[...])
    embed = (parts[:, :EMB] + parts[:, EMB:] + low[:, :EMB]).T
    packed = jnp.concatenate([embed[: EMB // 2], embed[EMB // 2 :]], axis=1)
    for n in range(PLACES):
        part1[n] = packed[2 * n : 2 * n + 2]
    pl.semaphore_wait(ready.at[0], len(relays))
    slot = y * PLACES + place
    send(1, other_y, slot, lambda there: part1.at[there], recv1)
    recv1[pl.ds(slot, 1)] = part1[pl.ds(place, 1)]
    for device in second:
        pl.semaphore_signal(ready.at[1], inc=1, device_id=device)

    inner_back(spec_g, spec_f, spec_y, inner)
    for b, conv in enumerate(gather(spec_y, turn)):
        send_s[b] = (conv + gain * recv_g[b].astype(F32)).astype(BF16)
    send(2, other_blocks, me, lambda there: send_s.at[there], recv_s)
    recv_s[pl.ds(me, 1)] = send_s[pl.ds(me, 1)]

    parts = dot(bg[: 2 * OWN], active[...], ((1,), (1,)))
    fgrad = (parts[:OWN, :HID] + parts[:OWN, HID:] + parts[OWN:, :HID]) * (1.0 / LENGTH)
    send_f[0] = jnp.concatenate([fgrad[: OWN // 2], fgrad[OWN // 2 :]], axis=1)
    send(4, other_blocks, me, lambda there: send_f.at[0], recv_f)
    recv_f[pl.ds(me, 1)] = send_f[...]

    wait(recv_sem, 1, recv1, RING * PLACES - 1)
    part2[...] = fold(recv1[...]) * (1.0 / math.sqrt(LENGTH))
    slot = place * RING + z
    pl.semaphore_wait(ready.at[1], len(second))
    send(3, other_z, slot, lambda there: part2.at[0], recv2)
    recv2[pl.ds(slot, 1)] = part2[...]

    wait(recv_sem, 2, recv_s, BLOCKS - 1)
    sig_out[...] = recv_s[...].astype(F32).reshape(BLOCKS * OWN, ROWS).T.astype(BF16)

    wait(recv_sem, 4, recv_f, BLOCKS - 1)
    pieces = recv_f[...]
    fgrad_out[...] = (
        jnp.concatenate([pieces[:, :, :HID], pieces[:, :, HID:]], axis=1).reshape(BLOCKS * OWN, HID).T
    )

    wait(send_sem, 0, send_u, BLOCKS - 1)
    wait(send_sem, 5, send_g, BLOCKS - 1)
    wait(send_sem, 1, recv1, RING * PLACES - 1)
    wait(send_sem, 2, send_s, BLOCKS - 1)
    wait(send_sem, 3, recv2, RING * PLACES - 1)
    wait(send_sem, 4, recv_f, BLOCKS - 1)

    wait(recv_sem, 3, recv2, RING * PLACES - 1)
    for n in range(PLACES):
        piece = fold(recv2[n * RING : (n + 1) * RING])[0]
        egrad_out[2 * n : 2 * n + 2] = piece[:, :HID]
        egrad_out[EMB // 2 + 2 * n : EMB // 2 + 2 * n + 2] = piece[:, HID:]


def hand_over(*refs):
    copies = [pltpu.make_async_copy(refs[n], refs[3 + n], refs[6].at[n]) for n in range(3)]
    for copy in copies:
        copy.start()
    for copy in copies:
        copy.wait()


def local(inputs, out_grad, embed_weight, filter_weight, decay_rate, skip_gain):
    channels = inputs.shape[1]
    feats, columns, inner, turn = tables()
    operands = (
        inputs,
        out_grad,
        embed_weight,
        filter_weight,
        decay_rate.reshape(1, channels),
        skip_gain.reshape(1, channels),
        jnp.asarray(feats),
        jnp.asarray(columns),
        jnp.asarray(inner),
        jnp.asarray(turn),
    )
    vmem = pltpu.VMEM
    results = pl.pallas_call(
        kernel,
        out_shape=(
            pltpu.VMEM((ROWS, channels), BF16),
            pltpu.VMEM((HID, channels), F32),
            pltpu.VMEM((EMB, HID), F32),
        ),
        in_specs=[pl.BlockSpec(memory_space=pltpu.HBM)] * len(operands),
        out_specs=[pl.BlockSpec(memory_space=pltpu.VMEM)] * 3,
        scratch_shapes=[vmem(x.shape, x.dtype) for x in operands]
        + [
            vmem((BLOCKS, OWN, ROWS), BF16),
            vmem((BLOCKS, OWN, ROWS), BF16),
            vmem((BLOCKS, OWN, ROWS), BF16),
            vmem((BLOCKS, OWN, ROWS), BF16),
            vmem((channels, ROWS), F32),
            vmem((HID, LENGTH), F32),
            vmem((2 * HID, LENGTH), BF16),
            vmem((HID, LENGTH), F32),
            vmem((2 * OWN, LENGTH), F32),
            vmem((BLOCKS, OWN, ROWS), F32),
            vmem((BLOCKS, OWN, ROWS), F32),
            vmem((KEPT, OWN, 2 * ROWS), F32),
            vmem((KEPT, OWN, 2 * ROWS), F32),
            vmem((KEPT, OWN, 2 * ROWS), F32),
            vmem((KEPT, OWN, 2 * ROWS), F32),
            vmem((4 * OWN, LENGTH), BF16),
            vmem((HID, 4 * OWN), BF16),
            vmem((BLOCKS, OWN, ROWS), BF16),
            vmem((BLOCKS, OWN, ROWS), BF16),
            vmem((1, OWN // 2, ROWS), F32),
            vmem((BLOCKS, OWN // 2, ROWS), F32),
            vmem((PLACES, 2, ROWS), F32),
            vmem((RING * PLACES, 2, ROWS), F32),
            vmem((1, 2, ROWS), F32),
            vmem((RING * PLACES, 2, ROWS), F32),
            pltpu.SemaphoreType.DMA((len(operands),)),
            pltpu.SemaphoreType.DMA((6,)),
            pltpu.SemaphoreType.DMA((6,)),
            pltpu.SemaphoreType.REGULAR((2,)),
        ],
        compiler_params=pltpu.CompilerParams(
            collective_id=0, has_side_effects=True, vmem_limit_bytes=40 * 1024 * 1024
        ),
        name="hyena_backward",
    )(*(pltpu.with_memory_space_constraint(x, pltpu.HBM) for x in operands))
    return pl.pallas_call(
        hand_over,
        out_shape=[jax.ShapeDtypeStruct(x.shape, x.dtype) for x in results],
        in_specs=[pl.BlockSpec(memory_space=pltpu.VMEM)] * 3,
        out_specs=[pl.BlockSpec(memory_space=pl.ANY)] * 3,
        scratch_shapes=[pltpu.SemaphoreType.DMA((3,))],
        name="hand_over",
    )(*(pltpu.with_memory_space_constraint(x, pltpu.VMEM) for x in results))


def solution(mesh):
    return jax.shard_map(
        local,
        mesh=mesh,
        in_specs=(P("seq", "ch"), P("seq", "ch"), P(), P(None, "ch"), P("ch"), P("ch")),
        out_specs=(P("seq", "ch"), P(None, "ch"), P()),
        check_vma=False,
    )
```
